32 devices in a mesh: dp: 16 (over z, x, core), pipe: 2 (over y).
Axes of the slice: x: 2, y: 2, z: 4, core: 2. Of those that a mesh axis runs over, the one named last changes fastest.
Arguments:
- block_input: bfloat16 [2, 4096, 1536], P('pipe', 'dp'), may hold values from -100 to 100
- saved_qkv: bfloat16 [2, 4096, 4608], P('pipe', 'dp'), may hold values from -10 to 10
- cotangent: bfloat16 [2, 4096, 1536], P('pipe', 'dp'), may hold values from -6 to 6
- mod_table: float32 [2, 3, 1536], P('pipe'), may hold values from -3 to 3
- clip_condition: float32 [2, 128, 4608], P('pipe', 'dp'), may hold values from -3 to 3
- clip_frames: int32 [2, 128], P('pipe', 'dp'), may hold values from 0 to 8, as said below
- frame_tokens: int32 [2, 128], P('pipe', 'dp'), may hold values from 2 to 64, as said below
- tile_layout: int32 [2, 32, 2], P('pipe', 'dp'), may hold values from 0 to 1, as said below
- frozen_qkv: bfloat16 [2, 1536, 4608], P('pipe', 'dp'), may hold values from -0.15625 to 0.15625
- frozen_out: bfloat16 [2, 1536, 1536], P('pipe', 'dp'), may hold values from -0.15625 to 0.15625
- adapters: bfloat16 [2, 9216, 128], P('pipe'), may hold values from -0.15625 to 0.15625
Outputs:
- upstream: bfloat16 [2, 4096, 1536], P('pipe', 'dp')
- d_table: float32 [2, 3, 1536], P('pipe')
- d_adapters: float32 [2, 9216, 128], P('pipe', 'dp')
The draws below stay inside these ranges and needn't reach their ends.
Inputs may be any that keep to these rules, and one draw needn't show every extreme that they name: `clip_frames`: clips are packed in slot order; a slot with 0 frames holds no clip and so does every later slot of that device; the clips of one device hold at most 256 tokens. `frame_tokens`: even. `tile_layout`: every diagonal tile is live.
All inputs are finite; a program needn't handle non-finite values.
Results may differ from the reference program's by a relative error of at most 0.0065.
Values may be sent and summed in bfloat16 or wider, within the bound.
No kernel may reach another device: no remote copies, remote signals or barrier semaphores. Data moves between devices by JAX's collectives and lax.ppermute only.
A program may use at most 128 MiB of HBM per device.

```python
import math
import jax
import jax.numpy as jnp
from jax import lax

D = 1536
HEADS = 12
HEAD = 128
RANK = 128
TOK_DEV = 256
TILE = 128
CLIPS = 8
FRAME_MAX = 8
PER_FRAME_MAX = 64
SECTIONS = 2
TOKENS = 4096
HD = 1536
TILES = 2
TILE_ROWS = 32
CLIP_SLOTS = 128
ADAPT_ROWS = 9216
N_DP = 16


def clip_plan(key):
    frame_key = jax.random.fold_in(key, 31)
    size_key = jax.random.fold_in(key, 37)
    grid = (SECTIONS, CLIP_SLOTS // CLIPS, CLIPS)
    counts = jax.random.randint(frame_key, grid, 1, FRAME_MAX + 1)
    widths = 2 * jax.random.randint(size_key, grid, 1, PER_FRAME_MAX // 2 + 1)
    clip_ends = jnp.cumsum(counts * widths, axis=2)
    kept = jnp.where(clip_ends <= TOK_DEV, counts, 0)
    return (kept.reshape(SECTIONS, CLIP_SLOTS).astype(jnp.int32), widths.reshape(SECTIONS, CLIP_SLOTS).astype(jnp.int32))


def draw_clip_frames(key, part):
    return clip_plan(key)[0]


def draw_frame_tokens(key, part):
    return clip_plan(key)[1]


def draw_tile_layout(key, part):
    grid = (SECTIONS, TILE_ROWS // TILES, TILES, TILES)
    random_live = jax.random.randint(key, grid, 0, 2)
    diagonal = (jnp.arange(TILES)[:, None] == jnp.arange(TILES)[None, :]).astype(jnp.int32)
    return jnp.maximum(random_live, diagonal[None, None]).reshape(SECTIONS, TILE_ROWS, TILES).astype(jnp.int32)


def draw_block_input(key, part):
    shape = (SECTIONS, TOKENS, D)
    row_scale = jnp.exp(jax.random.uniform(jax.random.fold_in(key, 3), (SECTIONS, TOKENS, 1), jnp.float32, math.log(0.5), math.log(5.0)))
    column_scale = jnp.exp(jax.random.uniform(jax.random.fold_in(key, 4), (SECTIONS, 1, D), jnp.float32, math.log(0.5), math.log(5.0)))
    base = jnp.clip(jax.random.normal(jax.random.fold_in(key, 7), shape, jnp.float32), -4.0, 4.0)
    return (base * row_scale * column_scale).astype(jnp.bfloat16)


def draw_saved_qkv(key, part):
    shape = (SECTIONS, TOKENS, 3, HEADS, HEAD)
    result = jnp.clip(jax.random.normal(jax.random.fold_in(key, 8), shape, jnp.float32), -4.0, 4.0)
    return result.reshape(SECTIONS, TOKENS, 3 * HEADS * HEAD).astype(jnp.bfloat16)


def shard_levels(rng, extent, shards, smallest, largest):
    def one(dim, blocks):
        heights = jax.random.uniform(jax.random.fold_in(jax.random.fold_in(rng, 6), dim), (blocks,), jnp.float32, smallest / len(shards), largest / len(shards))
        return jnp.repeat(jnp.exp(heights), extent[dim] // blocks).reshape((-1,) + (1,) * (len(extent) - dim - 1))

    loudness = one(*shards[0])
    for cut in shards[1:]:
        loudness = loudness * one(*cut)
    return loudness


def noise(key, shape, deviation, most, shards=(), held_as=jnp.bfloat16):
    factor_of = shard_levels(key, shape, shards, -0.22, 0.18) if shards else 1.0
    values = jax.random.normal(key, shape, jnp.float32) * deviation * factor_of
    return jnp.minimum(jnp.maximum(values, -most), most).astype(held_as)


def setup_inputs(seed: int = 0) -> dict:
    streams_of = jax.random.split(jax.random.key(seed), 12)
    block_input = draw_block_input(jax.random.fold_in(streams_of[11], 71), 0)
    saved_qkv = draw_saved_qkv(jax.random.fold_in(streams_of[11], 71), 0)
    cotangent = noise(streams_of[2], (SECTIONS, TOKENS, D), 1.0, 6.0, ((0, 2), (1, 16)))
    mod_table = noise(streams_of[3], (SECTIONS, 3, D), 0.5, 3.0, ((0, 2),), jnp.float32)
    clip_condition = noise(streams_of[4], (SECTIONS, CLIP_SLOTS, 3 * D), 0.5, 3.0, ((0, 2), (1, 16)), jnp.float32)
    clip_frames = draw_clip_frames(jax.random.fold_in(streams_of[11], 71), 0)
    frame_tokens = draw_frame_tokens(jax.random.fold_in(streams_of[11], 71), 0)
    tile_layout = draw_tile_layout(jax.random.fold_in(streams_of[11], 71), 0)
    frozen_qkv = noise(streams_of[8], (SECTIONS, D, 3 * HD), D ** -0.5, 0.15625, ((0, 2), (1, 16)))
    frozen_out = noise(streams_of[9], (SECTIONS, HD, D), HD ** -0.5, 0.15625, ((0, 2), (1, 16)))
    adapters = noise(streams_of[10], (SECTIONS, ADAPT_ROWS, RANK), D ** -0.5, 0.15625, ((0, 2),))
    return dict(block_input=block_input, saved_qkv=saved_qkv, cotangent=cotangent, mod_table=mod_table, clip_condition=clip_condition, clip_frames=clip_frames, frame_tokens=frame_tokens, tile_layout=tile_layout, frozen_qkv=frozen_qkv, frozen_out=frozen_out, adapters=adapters)


EPSILON = 1e-06
HIGH = lax.Precision.HIGHEST

def clip_index(frame_counts, frame_sizes, rows):
    clip_ends = jnp.cumsum(frame_counts * frame_sizes).astype(jnp.int32)
    position = jnp.arange(rows, dtype=jnp.int32)
    return lax.optimization_barrier(jnp.sum((position[:, None] >= clip_ends[None, :]).astype(jnp.int32), axis=1))

def device_terms(tokens_here, saved, cotangent_here, condition, frame_counts, frame_sizes, layout, table, frozen_in, frozen_back, adapter_rows):
    rows = tokens_here.shape[0]
    down_qkv = adapter_rows[:D]
    up_qkv = adapter_rows[D:D + 3 * HD]
    down_out = adapter_rows[D + 3 * HD:D + 4 * HD]
    up_out = adapter_rows[D + 4 * HD:]
    clip_of = clip_index(frame_counts, frame_sizes, rows)
    onehot_clip = (clip_of[:, None] == jnp.arange(CLIPS, dtype=jnp.int32)[None, :]).astype(jnp.float32)
    modulation = table.reshape(1, 3 * D) + jnp.dot(onehot_clip, condition, precision=HIGH)
    shift_rows = modulation[:, :D]
    scale_rows = modulation[:, D:2 * D]
    gate_rows = modulation[:, 2 * D:]
    inputs_f = tokens_here.astype(jnp.float32)
    centered = inputs_f - lax.optimization_barrier(jnp.mean(inputs_f, axis=1, keepdims=True))
    inverse = lax.rsqrt(lax.optimization_barrier(jnp.mean(centered * centered, axis=1, keepdims=True)) + EPSILON)
    normed = centered * inverse
    modded = (normed * (1.0 + scale_rows) + shift_rows).astype(jnp.bfloat16)
    position = jnp.arange(rows, dtype=jnp.int32)
    tile_of = position // TILE
    live_pairs = layout[tile_of][:, tile_of] > 0
    allowed = live_pairs & (clip_of[:, None] == clip_of[None, :])
    queries = saved[:, :HD].reshape(rows, HEADS, HEAD).astype(jnp.float32)
    key_rows = saved[:, HD:2 * HD].reshape(rows, HEADS, HEAD).astype(jnp.float32)
    value_rows = saved[:, 2 * HD:].reshape(rows, HEADS, HEAD).astype(jnp.float32)
    factor = HEAD ** (-0.5)
    scores = jnp.einsum('qhd,khd->hqk', queries, key_rows) * factor
    scores = jnp.where(allowed[None], scores, -jnp.inf)
    probs = jax.nn.softmax(scores, axis=2)
    probs_b = probs.astype(jnp.bfloat16).astype(jnp.float32)
    attention = jnp.einsum('hqk,khd->qhd', probs_b, value_rows).reshape(rows, HD).astype(jnp.bfloat16)
    low_out = jnp.dot(attention, down_out, preferred_element_type=jnp.float32).astype(jnp.bfloat16)
    branch = jnp.dot(attention, frozen_back, preferred_element_type=jnp.float32) + jnp.dot(low_out, up_out.T, preferred_element_type=jnp.float32)
    cotangent_f = cotangent_here.astype(jnp.float32)
    gated = (gate_rows * cotangent_f).astype(jnp.bfloat16)
    low_grad_out = jnp.dot(gated, up_out, preferred_element_type=jnp.float32).astype(jnp.bfloat16)
    grad_attention = (jnp.dot(gated, frozen_back.T, preferred_element_type=jnp.float32) + jnp.dot(low_grad_out, down_out.T, preferred_element_type=jnp.float32)).astype(jnp.bfloat16)
    grad_heads = grad_attention.reshape(rows, HEADS, HEAD).astype(jnp.float32)
    grad_probs = jnp.einsum('qhd,khd->hqk', grad_heads, value_rows)
    delta = lax.optimization_barrier(jnp.sum(probs * grad_probs, axis=2, keepdims=True))
    grad_scores = (probs * (grad_probs - delta) * factor).astype(jnp.bfloat16).astype(jnp.float32)
    grad_query = jnp.einsum('hqk,khd->qhd', grad_scores, key_rows).reshape(rows, HD)
    grad_key = jnp.einsum('hqk,qhd->khd', grad_scores, queries).reshape(rows, HD)
    grad_value = jnp.einsum('hqk,qhd->khd', probs_b, grad_heads).reshape(rows, HD)
    grad_qkv = jnp.concatenate([grad_query, grad_key, grad_value], axis=1).astype(jnp.bfloat16)
    low_in = jnp.dot(modded, down_qkv, preferred_element_type=jnp.float32).astype(jnp.bfloat16)
    low_grad_in = jnp.dot(grad_qkv, up_qkv, preferred_element_type=jnp.float32).astype(jnp.bfloat16)
    grad_modded = jnp.dot(grad_qkv, frozen_in.T, preferred_element_type=jnp.float32) + jnp.dot(low_grad_in, down_qkv.T, preferred_element_type=jnp.float32)
    grad_normed = grad_modded * (1.0 + scale_rows)
    grad_input = cotangent_f + inverse * (grad_normed - lax.optimization_barrier(jnp.mean(grad_normed, axis=1, keepdims=True)) - normed * lax.optimization_barrier(jnp.mean(grad_normed * normed, axis=1, keepdims=True)))
    table_part = jnp.stack([lax.optimization_barrier(jnp.sum(grad_modded, axis=0)), lax.optimization_barrier(jnp.sum(grad_modded * normed, axis=0)), lax.optimization_barrier(jnp.sum(cotangent_f * branch, axis=0))])
    adapter_part = jnp.concatenate([jnp.dot(modded.T, low_grad_in, preferred_element_type=jnp.float32), jnp.dot(grad_qkv.T, low_in, preferred_element_type=jnp.float32), jnp.dot(attention.T, low_grad_out, preferred_element_type=jnp.float32), jnp.dot(gated.T, low_out, preferred_element_type=jnp.float32)], axis=0)
    return (grad_input.astype(jnp.bfloat16), table_part, adapter_part)

def reference(block_input, saved_qkv, cotangent, mod_table, clip_condition, clip_frames, frame_tokens, tile_layout, frozen_qkv, frozen_out, adapters):
    grads_list = []
    table_list = []
    adapter_list = []
    for section in range(SECTIONS):

        def one_device(carry, pieces):
            table_acc, adapter_acc = carry
            grad_here, table_part, adapter_part = device_terms(pieces[0], pieces[1], pieces[2], pieces[3], pieces[4], pieces[5], pieces[6], mod_table[section], frozen_qkv[section], frozen_out[section], adapters[section])
            return ((table_acc + table_part, adapter_acc + adapter_part), grad_here)
        pieces = (block_input[section].reshape(N_DP, TOK_DEV, D), saved_qkv[section].reshape(N_DP, TOK_DEV, 3 * HD), cotangent[section].reshape(N_DP, TOK_DEV, D), clip_condition[section].reshape(N_DP, CLIPS, 3 * D), clip_frames[section].reshape(N_DP, CLIPS), frame_tokens[section].reshape(N_DP, CLIPS), tile_layout[section].reshape(N_DP, TILES, TILES))
        start_sums = (jnp.zeros((3, D), jnp.float32), jnp.zeros((ADAPT_ROWS, RANK), jnp.float32))
        (table_sum, adapter_sum), grads = lax.scan(one_device, start_sums, pieces)
        grads_list.append(grads.reshape(TOKENS, D))
        table_list.append(table_sum / N_DP)
        adapter_list.append(adapter_sum / N_DP)
    upstream = jnp.roll(jnp.stack(grads_list), -1, axis=0)
    return (upstream, jnp.stack(table_list), jnp.stack(adapter_list))
```

```python
import jax
import jax.numpy as jnp
from jax import lax
from jax.sharding import PartitionSpec as P

HEAD = 128
TILE = 128


EPSILON = 1e-06
HIGH = lax.Precision.HIGHEST


def contract_last(left, right):
    return lax.dot_general(
        left, right, (((1,), (1,)), ((), ())), preferred_element_type=jnp.float32
    )


def contract_first(left, right):
    return lax.dot_general(
        left, right, (((0,), (0,)), ((), ())), preferred_element_type=jnp.float32
    )


def swapped(block, bit):
    devices = range(lax.axis_size("dp"))
    return lax.ppermute(block, "dp", [(i, i ^ bit) for i in devices])


def ring_shifted(block):
    count = lax.axis_size("dp")
    return lax.ppermute(block, "dp", [(i, (i + 4) % count) for i in range(count)])


def lane_gather(block):
    me = lax.axis_index("dp")
    count = lax.axis_size("dp")
    rows, columns = block.shape
    whole = jnp.zeros((count // 2 * rows, columns), block.dtype)
    here = block
    for step in range(count // 4):
        if step:
            here = ring_shifted(here)
        across = swapped(here, 2)
        chip = (me - 4 * step + count) % count // 2
        whole = lax.dynamic_update_slice(whole, here, (chip * rows, 0))
        whole = lax.dynamic_update_slice(whole, across, ((chip ^ 1) * rows, 0))
    return whole


def interleaved(mine, other, lane, rows):
    first = jnp.where(lane == 0, mine, other)
    second = jnp.where(lane == 0, other, mine)
    columns = mine.shape[1]
    both = jnp.stack([first.reshape(-1, rows, columns), second.reshape(-1, rows, columns)], axis=1)
    return both.reshape(-1, columns)


def scatter_sum(part):
    me = lax.axis_index("dp")
    count = lax.axis_size("dp")
    rows, columns = part.shape
    kept = part.reshape(count, rows // count, columns)
    bit = 1
    while bit < count:
        mine = (me // bit) % 2
        pairs = kept.reshape(-1, 2, rows // count, columns)
        sent = lax.dynamic_index_in_dim(pairs, 1 - mine, 1, keepdims=False).astype(jnp.bfloat16)
        kept = lax.dynamic_index_in_dim(pairs, mine, 1, keepdims=False)
        kept = kept + swapped(sent, bit).astype(jnp.float32)
        bit *= 2
    return kept[0]


def whole_sum(part):
    bit = 1
    while bit < lax.axis_size("dp"):
        part = part + swapped(part, bit)
        bit *= 2
    return part


def on_device(
    block_input,
    saved_qkv,
    cotangent,
    mod_table,
    clip_condition,
    clip_frames,
    frame_tokens,
    tile_layout,
    frozen_qkv,
    frozen_out,
    adapters,
):
    lane = lax.axis_index("dp") % 2
    tokens_here = block_input[0]
    rows, width = tokens_here.shape
    saved = saved_qkv[0]
    inner = saved.shape[1] // 3
    heads = inner // HEAD
    slots = clip_frames.shape[1]
    tiles = tile_layout.shape[1]
    adapter_rows = adapters[0]
    down_qkv = adapter_rows[:width]
    up_qkv = adapter_rows[width : width + 3 * inner]
    down_out = adapter_rows[width + 3 * inner : width + 4 * inner]
    up_out = adapter_rows[width + 4 * inner :]

    lane_out = lane_gather(frozen_out[0])
    out_whole = interleaved(lane_out, swapped(lane_out, 1), lane, frozen_out.shape[1])
    lane_qkv = lane_gather(frozen_qkv[0])

    clip_ends = jnp.cumsum(clip_frames[0] * frame_tokens[0])
    position = jnp.arange(rows, dtype=jnp.int32)
    clip_of = jnp.sum((position[:, None] >= clip_ends[None, :]).astype(jnp.int32), axis=1)
    onehot_clip = (clip_of[:, None] == jnp.arange(slots, dtype=jnp.int32)[None, :]).astype(
        jnp.float32
    )
    modulation = mod_table[0].reshape(1, 3 * width) + jnp.dot(
        onehot_clip, clip_condition[0], precision=HIGH
    )
    shift_rows = modulation[:, :width]
    scale_rows = modulation[:, width : 2 * width]
    gate_rows = modulation[:, 2 * width :]
    inputs_f = tokens_here.astype(jnp.float32)
    centered = inputs_f - jnp.mean(inputs_f, axis=1, keepdims=True)
    inverse = lax.rsqrt(jnp.mean(centered * centered, axis=1, keepdims=True) + EPSILON)
    normed = centered * inverse
    modded = (normed * (1.0 + scale_rows) + shift_rows).astype(jnp.bfloat16)
    tile_onehot = (
        (position // TILE)[:, None] == jnp.arange(tiles, dtype=jnp.int32)[None, :]
    ).astype(jnp.float32)
    live_rows = jnp.dot(tile_onehot, tile_layout[0].astype(jnp.float32), precision=HIGH)
    live_pairs = jnp.dot(live_rows, tile_onehot.T, precision=HIGH) > 0.5
    allowed = live_pairs & (clip_of[:, None] == clip_of[None, :])
    queries = saved[:, :inner].reshape(rows, heads, HEAD)
    key_rows = saved[:, inner : 2 * inner].reshape(rows, heads, HEAD)
    value_rows = saved[:, 2 * inner :].reshape(rows, heads, HEAD)
    factor = HEAD ** (-0.5)
    scores = (
        jnp.einsum("qhd,khd->hqk", queries, key_rows, preferred_element_type=jnp.float32) * factor
    )
    scores = jnp.where(allowed[None], scores, -jnp.inf)
    probs = jax.nn.softmax(scores, axis=2)
    probs_b = probs.astype(jnp.bfloat16)
    attention = (
        jnp.einsum("hqk,khd->qhd", probs_b, value_rows, preferred_element_type=jnp.float32)
        .reshape(rows, inner)
        .astype(jnp.bfloat16)
    )
    low_out = jnp.dot(attention, down_out, preferred_element_type=jnp.float32).astype(jnp.bfloat16)
    cotangent_f = cotangent[0].astype(jnp.float32)
    gated = (gate_rows * cotangent_f).astype(jnp.bfloat16)
    low_grad_out = jnp.dot(gated, up_out, preferred_element_type=jnp.float32).astype(jnp.bfloat16)
    low_in = jnp.dot(modded, down_qkv, preferred_element_type=jnp.float32).astype(jnp.bfloat16)
    branch = jnp.dot(attention, out_whole, preferred_element_type=jnp.float32) + contract_last(
        low_out, up_out
    )
    grad_attention = (
        contract_last(gated, out_whole) + contract_last(low_grad_out, down_out)
    ).astype(jnp.bfloat16)
    grad_heads = grad_attention.reshape(rows, heads, HEAD)
    grad_probs = jnp.einsum(
        "qhd,khd->hqk", grad_heads, value_rows, preferred_element_type=jnp.float32
    )
    delta = jnp.sum(probs * grad_probs, axis=2, keepdims=True)
    grad_scores = (probs * (grad_probs - delta) * factor).astype(jnp.bfloat16)
    grad_query = jnp.einsum(
        "hqk,khd->qhd", grad_scores, key_rows, preferred_element_type=jnp.float32
    ).reshape(rows, inner)
    grad_key = jnp.einsum(
        "hqk,qhd->khd", grad_scores, queries, preferred_element_type=jnp.float32
    ).reshape(rows, inner)
    grad_value = jnp.einsum(
        "hqk,qhd->khd", probs_b, grad_heads, preferred_element_type=jnp.float32
    ).reshape(rows, inner)
    grad_qkv = jnp.concatenate([grad_query, grad_key, grad_value], axis=1).astype(jnp.bfloat16)
    grad_beside = swapped(grad_qkv, 1)
    low_grad_in = jnp.dot(grad_qkv, up_qkv, preferred_element_type=jnp.float32).astype(jnp.bfloat16)
    adapter_part = jnp.concatenate(
        [
            contract_first(modded, low_grad_in),
            contract_first(grad_qkv, low_in),
            contract_first(attention, low_grad_out),
            contract_first(gated, low_out),
        ],
        axis=0,
    )
    replicas = lax.axis_size("dp")
    adapter_sum = scatter_sum(adapter_part)

    part_rows = frozen_qkv.shape[1]
    frozen_beside = swapped(contract_last(grad_beside, lane_qkv), 1)
    frozen_mine = contract_last(grad_qkv, lane_qkv)
    first = jnp.where(lane == 0, frozen_mine, frozen_beside).reshape(rows, -1, part_rows)
    second = jnp.where(lane == 0, frozen_beside, frozen_mine).reshape(rows, -1, part_rows)
    frozen_part = jnp.stack([first, second], axis=2).reshape(rows, width)
    grad_modded = frozen_part + contract_last(low_grad_in, down_qkv)
    grad_normed = grad_modded * (1.0 + scale_rows)
    grad_input = cotangent_f + inverse * (
        grad_normed
        - jnp.mean(grad_normed, axis=1, keepdims=True)
        - normed * jnp.mean(grad_normed * normed, axis=1, keepdims=True)
    )
    grad_input = grad_input.astype(jnp.bfloat16)
    table_part = jnp.stack(
        [
            jnp.sum(grad_modded, axis=0),
            jnp.sum(grad_modded * normed, axis=0),
            jnp.sum(cotangent_f * branch, axis=0),
        ]
    )
    stages = lax.axis_size("pipe")
    passed_back = lax.ppermute(
        grad_input, "pipe", [((i + 1) % stages, i) for i in range(stages)]
    )
    table_sum = whole_sum(table_part)
    return (passed_back[None], (table_sum / replicas)[None], (adapter_sum / replicas)[None])


def solution(mesh):
    placed = (
        P("pipe", "dp", None),
        P("pipe", "dp", None),
        P("pipe", "dp", None),
        P("pipe", None, None),
        P("pipe", "dp", None),
        P("pipe", "dp"),
        P("pipe", "dp"),
        P("pipe", "dp", None),
        P("pipe", "dp", None),
        P("pipe", "dp", None),
        P("pipe", None, None),
    )
    return jax.shard_map(
        on_device,
        mesh=mesh,
        in_specs=placed,
        out_specs=(P("pipe", "dp", None), P("pipe", None, None), P("pipe", "dp", None)),
        check_vma=False,
    )
```

```python
import jax
import jax.numpy as jnp
from jax import lax
from jax.experimental import pallas as pl
from jax.experimental.pallas import tpu as pltpu
from jax.sharding import PartitionSpec as P

HEAD = 128
TILE = 128


EPSILON = 1e-06
HIGH = lax.Precision.HIGHEST


def contract_last(left, right):
    return lax.dot_general(
        left, right, (((1,), (1,)), ((), ())), preferred_element_type=jnp.float32
    )


def contract_first(left, right):
    return lax.dot_general(
        left, right, (((0,), (0,)), ((), ())), preferred_element_type=jnp.float32
    )


def swapped(block, bit):
    devices = range(lax.axis_size("dp"))
    return lax.ppermute(block, "dp", [(i, i ^ bit) for i in devices])


def ring_shifted(block):
    count = lax.axis_size("dp")
    return lax.ppermute(block, "dp", [(i, (i + 4) % count) for i in range(count)])


def lane_gather(block):
    me = lax.axis_index("dp")
    count = lax.axis_size("dp")
    rows, columns = block.shape
    whole = jnp.zeros((count // 2 * rows, columns), block.dtype)
    here = block
    for step in range(count // 4):
        if step:
            here = ring_shifted(here)
        across = swapped(here, 2)
        chip = (me - 4 * step + count) % count // 2
        whole = lax.dynamic_update_slice(whole, here, (chip * rows, 0))
        whole = lax.dynamic_update_slice(whole, across, ((chip ^ 1) * rows, 0))
    return whole


def interleaved(mine, other, lane, rows):
    first = jnp.where(lane == 0, mine, other)
    second = jnp.where(lane == 0, other, mine)
    columns = mine.shape[1]
    both = jnp.stack([first.reshape(-1, rows, columns), second.reshape(-1, rows, columns)], axis=1)
    return both.reshape(-1, columns)


def scatter_sum(part):
    me = lax.axis_index("dp")
    count = lax.axis_size("dp")
    rows, columns = part.shape
    kept = part.reshape(count, rows // count, columns)
    bit = 1
    while bit < count:
        mine = (me // bit) % 2
        pairs = kept.reshape(-1, 2, rows // count, columns)
        sent = lax.dynamic_index_in_dim(pairs, 1 - mine, 1, keepdims=False).astype(jnp.bfloat16)
        kept = lax.dynamic_index_in_dim(pairs, mine, 1, keepdims=False)
        kept = kept + swapped(sent, bit).astype(jnp.float32)
        bit *= 2
    return kept[0]


def whole_sum(part):
    bit = 1
    while bit < lax.axis_size("dp"):
        part = part + swapped(part, bit)
        bit *= 2
    return part


def on_device_general(
    block_input,
    saved_qkv,
    cotangent,
    mod_table,
    clip_condition,
    clip_frames,
    frame_tokens,
    tile_layout,
    frozen_qkv,
    frozen_out,
    adapters,
):
    lane = lax.axis_index("dp") % 2
    tokens_here = block_input[0]
    rows, width = tokens_here.shape
    saved = saved_qkv[0]
    inner = saved.shape[1] // 3
    heads = inner // HEAD
    slots = clip_frames.shape[1]
    tiles = tile_layout.shape[1]
    adapter_rows = adapters[0]
    down_qkv = adapter_rows[:width]
    up_qkv = adapter_rows[width : width + 3 * inner]
    down_out = adapter_rows[width + 3 * inner : width + 4 * inner]
    up_out = adapter_rows[width + 4 * inner :]

    lane_out = lane_gather(frozen_out[0])
    out_whole = interleaved(lane_out, swapped(lane_out, 1), lane, frozen_out.shape[1])
    lane_qkv = lane_gather(frozen_qkv[0])

    clip_ends = jnp.cumsum(clip_frames[0] * frame_tokens[0])
    position = jnp.arange(rows, dtype=jnp.int32)
    clip_of = jnp.sum((position[:, None] >= clip_ends[None, :]).astype(jnp.int32), axis=1)
    onehot_clip = (clip_of[:, None] == jnp.arange(slots, dtype=jnp.int32)[None, :]).astype(
        jnp.float32
    )
    modulation = mod_table[0].reshape(1, 3 * width) + jnp.dot(
        onehot_clip, clip_condition[0], precision=HIGH
    )
    shift_rows = modulation[:, :width]
    scale_rows = modulation[:, width : 2 * width]
    gate_rows = modulation[:, 2 * width :]
    inputs_f = tokens_here.astype(jnp.float32)
    centered = inputs_f - jnp.mean(inputs_f, axis=1, keepdims=True)
    inverse = lax.rsqrt(jnp.mean(centered * centered, axis=1, keepdims=True) + EPSILON)
    normed = centered * inverse
    modded = (normed * (1.0 + scale_rows) + shift_rows).astype(jnp.bfloat16)
    tile_onehot = (
        (position // TILE)[:, None] == jnp.arange(tiles, dtype=jnp.int32)[None, :]
    ).astype(jnp.float32)
    live_rows = jnp.dot(tile_onehot, tile_layout[0].astype(jnp.float32), precision=HIGH)
    live_pairs = jnp.dot(live_rows, tile_onehot.T, precision=HIGH) > 0.5
    allowed = live_pairs & (clip_of[:, None] == clip_of[None, :])
    queries = saved[:, :inner].reshape(rows, heads, HEAD)
    key_rows = saved[:, inner : 2 * inner].reshape(rows, heads, HEAD)
    value_rows = saved[:, 2 * inner :].reshape(rows, heads, HEAD)
    factor = HEAD ** (-0.5)
    scores = (
        jnp.einsum("qhd,khd->hqk", queries, key_rows, preferred_element_type=jnp.float32) * factor
    )
    scores = jnp.where(allowed[None], scores, -jnp.inf)
    probs = jax.nn.softmax(scores, axis=2)
    probs_b = probs.astype(jnp.bfloat16)
    attention = (
        jnp.einsum("hqk,khd->qhd", probs_b, value_rows, preferred_element_type=jnp.float32)
        .reshape(rows, inner)
        .astype(jnp.bfloat16)
    )
    low_out = jnp.dot(attention, down_out, preferred_element_type=jnp.float32).astype(jnp.bfloat16)
    cotangent_f = cotangent[0].astype(jnp.float32)
    gated = (gate_rows * cotangent_f).astype(jnp.bfloat16)
    low_grad_out = jnp.dot(gated, up_out, preferred_element_type=jnp.float32).astype(jnp.bfloat16)
    low_in = jnp.dot(modded, down_qkv, preferred_element_type=jnp.float32).astype(jnp.bfloat16)
    branch = jnp.dot(attention, out_whole, preferred_element_type=jnp.float32) + contract_last(
        low_out, up_out
    )
    grad_attention = (
        contract_last(gated, out_whole) + contract_last(low_grad_out, down_out)
    ).astype(jnp.bfloat16)
    grad_heads = grad_attention.reshape(rows, heads, HEAD)
    grad_probs = jnp.einsum(
        "qhd,khd->hqk", grad_heads, value_rows, preferred_element_type=jnp.float32
    )
    delta = jnp.sum(probs * grad_probs, axis=2, keepdims=True)
    grad_scores = (probs * (grad_probs - delta) * factor).astype(jnp.bfloat16)
    grad_query = jnp.einsum(
        "hqk,khd->qhd", grad_scores, key_rows, preferred_element_type=jnp.float32
    ).reshape(rows, inner)
    grad_key = jnp.einsum(
        "hqk,qhd->khd", grad_scores, queries, preferred_element_type=jnp.float32
    ).reshape(rows, inner)
    grad_value = jnp.einsum(
        "hqk,qhd->khd", probs_b, grad_heads, preferred_element_type=jnp.float32
    ).reshape(rows, inner)
    grad_qkv = jnp.concatenate([grad_query, grad_key, grad_value], axis=1).astype(jnp.bfloat16)
    grad_beside = swapped(grad_qkv, 1)
    low_grad_in = jnp.dot(grad_qkv, up_qkv, preferred_element_type=jnp.float32).astype(jnp.bfloat16)
    adapter_part = jnp.concatenate(
        [
            contract_first(modded, low_grad_in),
            contract_first(grad_qkv, low_in),
            contract_first(attention, low_grad_out),
            contract_first(gated, low_out),
        ],
        axis=0,
    )
    replicas = lax.axis_size("dp")
    adapter_sum = scatter_sum(adapter_part)

    part_rows = frozen_qkv.shape[1]
    frozen_beside = swapped(contract_last(grad_beside, lane_qkv), 1)
    frozen_mine = contract_last(grad_qkv, lane_qkv)
    first = jnp.where(lane == 0, frozen_mine, frozen_beside).reshape(rows, -1, part_rows)
    second = jnp.where(lane == 0, frozen_beside, frozen_mine).reshape(rows, -1, part_rows)
    frozen_part = jnp.stack([first, second], axis=2).reshape(rows, width)
    grad_modded = frozen_part + contract_last(low_grad_in, down_qkv)
    grad_normed = grad_modded * (1.0 + scale_rows)
    grad_input = cotangent_f + inverse * (
        grad_normed
        - jnp.mean(grad_normed, axis=1, keepdims=True)
        - normed * jnp.mean(grad_normed * normed, axis=1, keepdims=True)
    )
    grad_input = grad_input.astype(jnp.bfloat16)
    table_part = jnp.stack(
        [
            jnp.sum(grad_modded, axis=0),
            jnp.sum(grad_modded * normed, axis=0),
            jnp.sum(cotangent_f * branch, axis=0),
        ]
    )
    stages = lax.axis_size("pipe")
    passed_back = lax.ppermute(
        grad_input, "pipe", [((i + 1) % stages, i) for i in range(stages)]
    )
    table_sum = whole_sum(table_part)
    return (passed_back[None], (table_sum / replicas)[None], (adapter_sum / replicas)[None])


VMEM_LIMIT = 58 * 1024 * 1024
PACE = 1.0e6
F32 = jnp.float32
BF16 = jnp.bfloat16


def dot_nn(left, right):
    return lax.dot_general(
        left, right, (((1,), (0,)), ((), ())), preferred_element_type=jnp.float32
    )


def clip_numbers(frames_ref, sizes_ref, position):
    clip = jnp.zeros_like(position)
    end = jnp.int32(0)
    for slot in range(frames_ref.shape[1]):
        end = end + frames_ref[0, slot] * sizes_ref[0, slot]
        clip = clip + (position >= end).astype(jnp.int32)
    return clip


def mask_bias(frames_ref, sizes_ref, layout_ref, rows):
    down = lax.broadcasted_iota(jnp.int32, (rows, 1), 0)
    across = lax.broadcasted_iota(jnp.int32, (1, rows), 1)
    same = clip_numbers(frames_ref, sizes_ref, down) == clip_numbers(frames_ref, sizes_ref, across)
    live = jnp.zeros((rows, rows), jnp.int32)
    for i in range(rows // TILE):
        for j in range(rows // TILE):
            inside = (across // TILE == i) & (down // TILE == j)
            live = jnp.where(inside, layout_ref[0, i, j], live)
    return jnp.where(same & (live > 0), 0.0, -jnp.inf).astype(jnp.float32)


def pre_kernel(
    place_ref, frames_ref, sizes_ref, input_ref, cotangent_ref, table_ref, condition_ref, adapters_ref,
    modded_ref, gated_ref, normed_ref, scale_ref, low_in_ref, low_grad_ref,
    down_ref, up_ref, sems,
):
    rows, width = input_ref.shape
    slots = condition_ref.shape[0]
    down = pltpu.make_async_copy(adapters_ref.at[0, :width, :], down_ref, sems.at[0])
    up = pltpu.make_async_copy(adapters_ref.at[0, adapters_ref.shape[1] - width :, :], up_ref, sems.at[1])
    down.start()
    up.start()
    position = lax.broadcasted_iota(jnp.int32, (rows, 1), 0)
    clip = clip_numbers(frames_ref, sizes_ref, position)
    whole = condition_ref[...]
    high = whole.astype(BF16)
    rest = whole - high.astype(F32)
    middle = rest.astype(BF16)
    low = (rest - middle.astype(F32)).astype(BF16)
    parts = jnp.concatenate([high.astype(F32), middle.astype(F32), low.astype(F32)], axis=0)
    lanes = lax.broadcasted_iota(jnp.int32, (rows, 3 * slots), 1) % slots
    onehot = (clip == lanes).astype(F32).astype(BF16)
    parts = parts.astype(BF16)

    def modulation(which):
        columns = slice(which * width, (which + 1) * width)
        return dot_nn(onehot, parts[:, columns]) + table_ref[which : which + 1, :]

    inputs_f = input_ref[...].astype(F32)
    centered = inputs_f - jnp.mean(inputs_f, axis=1, keepdims=True)
    inverse = lax.rsqrt(jnp.mean(centered * centered, axis=1, keepdims=True) + EPSILON)
    normed = centered * inverse
    normed_ref[...] = normed
    scale = 1.0 + modulation(1)
    scale_ref[...] = scale
    modded = (normed * scale + modulation(0)).astype(BF16)
    modded_ref[...] = modded
    gated = (modulation(2) * cotangent_ref[...].astype(F32)).astype(BF16)
    gated_ref[...] = gated
    down.wait()
    low_in_ref[...] = dot_nn(modded, down_ref[...]).astype(BF16)
    up.wait()
    low_grad_ref[...] = dot_nn(gated, up_ref[...]).astype(BF16)


def forward_kernel(
    place_ref, frames_ref, sizes_ref, layout_ref, low_grad_ref, saved_in_ref, gated_in_ref,
    cotangent_in_ref, adapters_ref, attention_ref, low_out_ref, gate_ref, grad_down_ref, grad_up_ref,
    bias_ref, level_ref, down_ref, up_ref, saved_ref, gated_ref, cotangent_ref, sems,
):
    rows, inner = attention_ref.shape
    width = up_ref.shape[0]
    count = adapters_ref.shape[1]
    down = pltpu.make_async_copy(
        adapters_ref.at[0, count - width - inner : count - width, :], down_ref, sems.at[0]
    )
    up = pltpu.make_async_copy(adapters_ref.at[0, count - width :, :], up_ref, sems.at[1])
    factor = HEAD ** (-0.5)
    group = 3
    held = []
    for n, start in enumerate(range(0, inner, group * HEAD)):
        stop = min(start + group * HEAD, inner)
        for part in range(3):
            columns = slice(part * inner + start, part * inner + stop)
            held.append(
                pltpu.make_async_copy(
                    saved_in_ref.at[:, columns], saved_ref.at[:, columns], sems.at[4 + 3 * n + part]
                )
            )
    gated_copy = pltpu.make_async_copy(gated_in_ref, gated_ref, sems.at[2])
    cotangent_copy = pltpu.make_async_copy(cotangent_in_ref, cotangent_ref, sems.at[3])
    for copy in held + [down, gated_copy, cotangent_copy, up]:
        copy.start()
    bias_ref[...] = mask_bias(frames_ref, sizes_ref, layout_ref, rows)
    for start in range(0, inner // HEAD, group):
        heads = range(start, min(start + group, inner // HEAD))
        for copy in held[start // group * 3 : start // group * 3 + 3]:
            copy.wait()
        scores = []
        for head in heads:
            query = saved_ref[:, head * HEAD : (head + 1) * HEAD]
            key = saved_ref[:, inner + head * HEAD : inner + (head + 1) * HEAD]
            scores.append(contract_last(key, query) * factor + bias_ref[...])
        probs = []
        for head, score in zip(heads, scores):
            most = jnp.max(score, axis=0, keepdims=True)
            raised = jnp.exp(score - most)
            whole = jnp.sum(raised, axis=0, keepdims=True)
            level_ref[head : head + 1, :] = most + jnp.log(whole)
            probs.append((raised * (1.0 / whole)).astype(BF16))
        for head, prob in zip(heads, probs):
            value = saved_ref[:, 2 * inner + head * HEAD : 2 * inner + (head + 1) * HEAD]
            attention_ref[:, head * HEAD : (head + 1) * HEAD] = contract_first(prob, value).astype(BF16)
    down.wait()
    attention = attention_ref[...]
    low_out = dot_nn(attention, down_ref[...]).astype(BF16)
    low_out_ref[...] = low_out
    grad_down_ref[...] = contract_first(attention, low_grad_ref[...])
    gated_copy.wait()
    grad_up_ref[...] = contract_first(gated_ref[...], low_out)
    up.wait()
    cotangent_copy.wait()
    branch = contract_last(low_out, up_ref[...])
    gate_ref[...] = jnp.sum(branch * cotangent_ref[...].astype(F32), axis=0, keepdims=True)


def layer_of(place_ref, step):
    ring = place_ref[2]
    return lax.rem(place_ref[0] - step + ring, ring)


def shard_copies(place_ref, shards, whole_ref, sems):
    copies = []
    for pieces, flip in zip(shards, (0, 2, 1, 3)):
        owner = (place_ref[1] ^ flip) * (whole_ref.shape[0] // 4)
        offset = 0
        for piece in pieces:
            start = pl.multiple_of(owner + offset, 16)
            offset += piece.shape[0]
            target = whole_ref.at[pl.ds(start, piece.shape[0]), :]
            copies.append(pltpu.make_async_copy(piece, target, sems.at[len(copies)]))
    return copies


def nested(refs, sizes):
    refs = list(refs)
    return [[refs.pop(0) for _ in range(size)] for size in sizes]


def backward_kernel(
    step, sizes,
    place_ref, low_grad_ref, low_in_ref, bias_ref, level_ref, gate_in_ref, total_in_ref,
    gated_in_ref, cotangent_in_ref, saved_ref, attention_ref, adapters_ref, *refs,
):
    shards = nested(refs, sizes)
    refs = refs[sum(sizes) :]
    grad_ref, grad_up_ref, gate_ref, total_ref = refs[:4]
    whole_ref, held_ref, out_ref, down_ref, up_ref, gated_ref, cotangent_ref, sems = refs[4:]
    depth, width = whole_ref.shape
    inner = attention_ref.shape[1]
    first = pl.multiple_of(layer_of(place_ref, step) * depth, HEAD)
    layer = pl.ds(first, depth)
    weights = shard_copies(place_ref, shards, whole_ref, sems)
    used = len(weights)
    parts = [pl.ds(pl.multiple_of(part * inner + first, HEAD), depth) for part in range(3)]
    held = [
        pltpu.make_async_copy(saved_ref.at[:, parts[part]], held_ref.at[part], sems.at[used + part])
        for part in range(3)
    ]
    others = [
        pltpu.make_async_copy(gated_in_ref, gated_ref, sems.at[used + 8]),
        pltpu.make_async_copy(cotangent_in_ref, cotangent_ref, sems.at[used + 9]),
        pltpu.make_async_copy(attention_ref.at[:, layer], out_ref, sems.at[used + 3]),
        pltpu.make_async_copy(
            adapters_ref.at[0, pl.ds(pl.multiple_of(width + 3 * inner + first, HEAD), depth), :],
            down_ref,
            sems.at[used + 4],
        ),
    ] + [
        pltpu.make_async_copy(
            adapters_ref.at[0, pl.ds(pl.multiple_of(width + part * inner + first, HEAD), depth), :],
            up_ref.at[pl.ds(part * depth, depth), :],
            sems.at[used + 5 + part],
        )
        for part in range(3)
    ]
    for copy in held + weights + others:
        copy.start()
    factor = HEAD ** (-0.5)
    heads = range(depth // HEAD)
    spans = [slice(head * HEAD, (head + 1) * HEAD) for head in heads]
    for copy in held:
        copy.wait()
    probs = []
    for head in heads:
        scores = contract_last(held_ref[1, :, spans[head]], held_ref[0, :, spans[head]]) * factor
        level = level_ref[pl.ds(layer_of(place_ref, step) * len(heads) + head, 1), :]
        probs.append(jnp.exp(scores + (bias_ref[...] - level)))
    for copy in weights + others:
        copy.wait()
    grad_attention = (
        contract_last(gated_ref[...], whole_ref[...])
        + contract_last(low_grad_ref[...], down_ref[...])
    ).astype(BF16)
    grad_scores = []
    for head in heads:
        grad = grad_attention[:, spans[head]]
        grad_probs = contract_last(held_ref[2, :, spans[head]], grad)
        delta = jnp.sum(probs[head] * grad_probs, axis=0, keepdims=True)
        grad_scores.append((probs[head] * ((grad_probs - delta) * factor)).astype(BF16))
    for head in heads:
        grad = grad_attention[:, spans[head]]
        pieces = (
            contract_first(grad_scores[head], held_ref[1, :, spans[head]]),
            dot_nn(grad_scores[head], held_ref[0, :, spans[head]]),
            dot_nn(probs[head].astype(BF16), grad),
        )
        for part, piece in enumerate(pieces):
            columns = slice(part * depth + head * HEAD, part * depth + (head + 1) * HEAD)
            grad_ref[:, columns] = piece.astype(BF16)
    grads = grad_ref[...]
    grad_up_ref[...] = contract_first(grads, low_in_ref[...])
    total_ref[...] = total_in_ref[...] + dot_nn(grads, up_ref[...])
    branch = dot_nn(out_ref[...], whole_ref[...])
    gate_ref[...] = gate_in_ref[...] + jnp.sum(
        branch * cotangent_ref[...].astype(F32), axis=0, keepdims=True
    )


def adapter_kernel(
    ring, place_ref, modded_ref, total_ref, grad_down_ref, grad_up_ref, *refs,
):
    layer_refs, (low_ref, sent_ref, kept_ref, whole_ref) = refs[:ring], refs[ring:]
    width = modded_ref.shape[1]
    inner = grad_down_ref.shape[0]
    depth = inner // ring
    low = total_ref[...].astype(BF16)
    low_ref[...] = low
    whole_ref[:width, :] = contract_first(modded_ref[...], low)
    for step in range(ring):
        first = layer_of(place_ref, step) * depth
        for part in range(3):
            start = pl.multiple_of(width + part * inner + first, HEAD)
            whole_ref[pl.ds(start, depth), :] = layer_refs[step][part * depth : (part + 1) * depth, :]
    whole_ref[width + 3 * inner : width + 4 * inner, :] = grad_down_ref[...]
    whole_ref[width + 4 * inner :, :] = grad_up_ref[...]
    blocks, block = kept_ref.shape[0], kept_ref.shape[1]
    lane = place_ref[1] % 2
    for j in range(blocks):
        mine = pl.multiple_of((2 * j + lane) * block, 64)
        other = pl.multiple_of((2 * j + 1 - lane) * block, 64)
        kept_ref[j] = whole_ref[pl.ds(mine, block), :]
        sent_ref[j] = whole_ref[pl.ds(other, block), :].astype(BF16)


def input_kernel(
    step, ring, sizes, place_ref, low_ref, *refs,
):
    grad_refs, refs = refs[:ring], refs[ring:]
    normed_ref, scale_ref, adapters_ref = refs[:3]
    shards = nested(refs[3:], sizes)
    u_ref, table_ref, whole_ref, near_ref, down_ref, held_ref, sems = refs[3 + sum(sizes) :]
    depth = whole_ref.shape[0]
    inner = whole_ref.shape[1] // 3
    weights = shard_copies(place_ref, shards, whole_ref, sems)
    used = len(weights)
    first = pl.multiple_of(layer_of(place_ref, step) * depth, HEAD)
    others = [
        pltpu.make_async_copy(adapters_ref.at[0, pl.ds(first, depth), :], down_ref, sems.at[used]),
        pltpu.make_async_copy(normed_ref.at[:, pl.ds(first, depth)], near_ref.at[0], sems.at[used + 1]),
        pltpu.make_async_copy(scale_ref.at[:, pl.ds(first, depth)], near_ref.at[1], sems.at[used + 2]),
    ]
    held = [
        pltpu.make_async_copy(grad_refs[n], held_ref.at[n], sems.at[used + 3 + n]) for n in range(ring)
    ]
    for copy in weights + held + others:
        copy.start()
    for copy in weights + others:
        copy.wait()
    total = contract_last(low_ref[...], down_ref[...])
    for other in range(ring):
        held[other].wait()
        start = layer_of(place_ref, other) * depth
        for part in range(3):
            columns = pl.ds(pl.multiple_of(part * inner + start, HEAD), depth)
            total = total + contract_last(
                held_ref[other, :, part * depth : (part + 1) * depth], whole_ref[:, columns]
            )
    u_ref[...] = (total * near_ref[1]).astype(BF16)
    table_ref[0:1, :] = jnp.sum(total, axis=0, keepdims=True)
    table_ref[1:2, :] = jnp.sum(total * near_ref[0], axis=0, keepdims=True)


def finish_kernel(ring, place_ref, input_ref, cotangent_ref, *refs):
    u_refs, (out_ref, u_ref) = refs[:ring], refs[ring:]
    depth = u_refs[0].shape[1]
    for step in range(ring):
        layer = pl.ds(pl.multiple_of(layer_of(place_ref, step) * depth, HEAD), depth)
        u_ref[:, layer] = u_refs[step][...].astype(F32)
    inputs_f = input_ref[...].astype(F32)
    centered = inputs_f - jnp.mean(inputs_f, axis=1, keepdims=True)
    inverse = lax.rsqrt(jnp.mean(centered * centered, axis=1, keepdims=True) + EPSILON)
    normed = centered * inverse
    u = u_ref[...]
    out_ref[...] = (
        cotangent_ref[...].astype(F32)
        + inverse
        * (
            u
            - jnp.mean(u, axis=1, keepdims=True)
            - normed * jnp.mean(u * normed, axis=1, keepdims=True)
        )
    ).astype(BF16)


def call(kernel, outs, specs, operands, time, scratch=(), name=None):
    space = {"s": pltpu.SMEM, "v": pltpu.VMEM, "a": pl.ANY}
    return pl.pallas_call(
        kernel,
        out_shape=outs,
        in_specs=[pl.BlockSpec(memory_space=space[s]) for s in specs],
        out_specs=[pl.BlockSpec(memory_space=pltpu.VMEM)] * len(outs),
        scratch_shapes=list(scratch),
        compiler_params=pltpu.CompilerParams(vmem_limit_bytes=VMEM_LIMIT),
        cost_estimate=pl.CostEstimate(flops=0, bytes_accessed=int(time * PACE), transcendentals=0),
        name=name,
    )(*operands)


def shape(*dims, dtype=BF16):
    return jax.ShapeDtypeStruct(dims, dtype)


def gate(value, *events):
    return lax.optimization_barrier((value, *events))[0]


def exchanged_sum(part, event):
    count = lax.axis_size("dp")
    total = part
    for flip in (1, 2, 3):
        total = total + swapped(part, flip)
    part = total
    for distance in range(4, count, 4):
        route = [(i, (i + distance) % count) for i in range(count)]
        total = total + gate(lax.ppermute(part, "dp", route), event)
    return total


def on_device(
    block_input,
    saved_qkv,
    cotangent,
    mod_table,
    clip_condition,
    clip_frames,
    frame_tokens,
    tile_layout,
    frozen_qkv,
    frozen_out,
    adapters,
):
    count = lax.axis_size("dp")
    depth = 4 * frozen_out.shape[1]
    if count != 16 or depth % HEAD or depth != 4 * frozen_qkv.shape[1]:
        return on_device_general(
            block_input, saved_qkv, cotangent, mod_table, clip_condition, clip_frames,
            frame_tokens, tile_layout, frozen_qkv, frozen_out, adapters,
        )
    ring = count // 4
    me = lax.axis_index("dp")
    place = jnp.stack([me // 4, me % 4, jnp.int32(ring)]).astype(jnp.int32)
    tokens_here, saved, cot = block_input[0], saved_qkv[0], cotangent[0]
    rows, width = tokens_here.shape
    inner = saved.shape[1] // 3
    rank = adapters.shape[2]
    heads = inner // HEAD
    stages = lax.axis_size("pipe")
    before = [((i + 1) % stages, i) for i in range(stages)]
    clips = [clip_frames, frame_tokens]
    beside = lambda block: swapped(block, 1)
    across = lambda block: swapped(block, 2)
    cut = frozen_qkv.shape[1] // 96 * 64

    out_r, qkv_r = [frozen_out[0]], [frozen_qkv[0]]
    out_r.append(ring_shifted(out_r[0]))
    out_x = [across(out_r[0])]
    out_rc, out_xc, qkv_x, qkv_rc, qkv_xc = [beside(out_r[0])], [], [], [], []
    modded, gated, normed, scale, low_in, low_grad_out = call(
        pre_kernel,
        [shape(rows, width), shape(rows, width), shape(rows, width, dtype=F32),
         shape(rows, width, dtype=F32), shape(rows, rank), shape(rows, rank)],
        "sssvvvva",
        [place, *clips, tokens_here, cot, mod_table[0], clip_condition[0], adapters],
        4,
        scratch=[pltpu.VMEM((width, rank), BF16), pltpu.VMEM((width, rank), BF16), pltpu.SemaphoreType.DMA((2,))],
        name="modulate",
    )
    event = low_in
    out_r.append(ring_shifted(gate(out_r[1], event)))
    out_x.append(across(gate(out_r[1], event)))
    out_xc.append(beside(gate(out_x[0], event)))
    attention, low_out, gate_sum, grad_down_out, grad_up_out, bias, level = call(
        forward_kernel,
        [shape(rows, inner), shape(rows, rank), shape(1, width, dtype=F32),
         shape(inner, rank, dtype=F32), shape(width, rank, dtype=F32),
         shape(rows, rows, dtype=F32), shape(heads, rows, dtype=F32)],
        "ssssvaaaa",
        [gate(place, out_r[1], out_x[0]), *clips, tile_layout, low_grad_out, saved, gated, cot, adapters],
        6,
        scratch=[
            pltpu.VMEM((inner, rank), BF16), pltpu.VMEM((width, rank), BF16),
            pltpu.VMEM(saved.shape, BF16), pltpu.VMEM((rows, width), BF16),
            pltpu.VMEM((rows, width), BF16), pltpu.SemaphoreType.DMA((4 + 3 * heads,)),
        ],
        name="attend",
    )

    event = low_out

    def backward(step, gate_sum, total, *waited):
        shards = ([out_r[step]], [out_x[step]], [out_rc[step]], [out_xc[step]])
        return call(
            lambda *refs: backward_kernel(step, [1, 1, 1, 1], *refs),
            [shape(rows, 3 * depth), shape(3 * depth, rank, dtype=F32),
             shape(1, width, dtype=F32), shape(rows, rank, dtype=F32)],
            "svvvvvvaaaaaaaaa",
            [gate(place, *waited), low_grad_out, low_in, bias, level, gate_sum, total, gated, cot, saved,
             attention, adapters, *sum(shards, [])],
            5,
            scratch=[
                pltpu.VMEM((depth, width), BF16), pltpu.VMEM((3, rows, depth), BF16),
                pltpu.VMEM((rows, depth), BF16), pltpu.VMEM((depth, rank), BF16),
                pltpu.VMEM((3 * depth, rank), BF16), pltpu.VMEM((rows, width), BF16),
                pltpu.VMEM((rows, width), BF16), pltpu.SemaphoreType.DMA((14,)),
            ],
            name=f"backward{step}",
        )

    total = jnp.zeros((rows, rank), F32)
    out_r.append(ring_shifted(gate(out_r[2], event)))
    out_x.append(across(gate(out_r[2], event)))
    out_rc.append(beside(gate(out_r[1], event)))
    out_xc.append(beside(gate(out_x[1], event)))
    grad0, grad_up0, gate_sum, total = backward(0, gate_sum, total, out_r[2], out_x[1], out_xc[0])
    event = total
    out_x.append(across(gate(out_r[3], event)))
    qkv_r.append(ring_shifted(gate(qkv_r[0], event, out_r[3])))
    qkv_rc.append(beside(gate(qkv_r[0], event)))
    out_rc.append(beside(gate(out_r[2], event)))
    out_xc.append(beside(gate(out_x[2], event)))
    grad1, grad_up1, gate_sum, total = backward(1, gate_sum, total, out_r[3], out_x[2])
    event = total
    qkv_x.append(across(gate(qkv_r[0], event, out_x[3])))
    out_rc.append(beside(gate(out_r[3], event)))
    out_xc.append(beside(gate(out_x[3], event)))
    grad2, grad_up2, gate_sum, total = backward(2, gate_sum, total, out_x[3])
    grad3, grad_up3, gate_sum, total = backward(3, gate_sum, total)
    event = total
    grads = [grad0, grad1, grad2, grad3]
    grad_ups = [grad_up0, grad_up1, grad_up2, grad_up3]

    block = adapters.shape[1] // count
    low_grad_in, sent, kept = call(
        lambda *refs: adapter_kernel(ring, *refs),
        [shape(rows, rank), shape(count // 2, block, rank), shape(count // 2, block, rank, dtype=F32)],
        "svvvv" + "v" * ring,
        [place, modded, total, grad_down_out, grad_up_out, *grad_ups],
        4,
        scratch=[pltpu.VMEM(adapters.shape[1:], F32)],
        name="adapt",
    )

    def project(step, *waited):
        shards = layers[step]
        sizes = [len(shard) for shard in shards]
        return call(
            lambda *refs: input_kernel(step, ring, sizes, *refs),
            [shape(rows, depth), shape(2, depth, dtype=F32)],
            "sv" + "a" * ring + "aaa" + "a" * sum(sizes),
            [gate(place, *waited), low_grad_in, *grads, normed, scale, adapters, *sum(shards, [])],
            5,
            scratch=[
                pltpu.VMEM((depth, 3 * inner), BF16), pltpu.VMEM((2, rows, depth), F32),
                pltpu.VMEM((depth, rank), BF16), pltpu.VMEM((ring, rows, 3 * depth), BF16),
                pltpu.SemaphoreType.DMA((9 + ring,)),
            ],
            name=f"project{step}",
        )

    def halved(kept, bit):
        mine = (me // bit) % 2
        pairs = kept.reshape(-1, 2, block, rank)
        sent = lax.dynamic_index_in_dim(pairs, 1 - mine, 1, keepdims=False).astype(BF16)
        return lax.dynamic_index_in_dim(pairs, mine, 1, keepdims=False), sent

    sends = lambda u: lax.ppermute(u, "pipe", before)
    event = low_grad_in
    qkv_r.append(ring_shifted(gate(qkv_r[1], event)))
    qkv_x.append(across(gate(qkv_r[1], event)))
    qkv_rc.append(beside(gate(qkv_r[1], event)))
    qkv_xc.append(beside(gate(qkv_x[0], event)))
    arrived = beside(sent)
    layers = [[[qkv_r[0]], [qkv_x[0]], [qkv_rc[0]], [qkv_xc[0]]]]
    u0, table0 = project(0, qkv_xc[0])
    qkv_r.append(ring_shifted(gate(qkv_r[2], u0)))
    qkv_x.append(across(gate(qkv_r[2], u0)))
    qkv_rc.append(beside(gate(qkv_r[2], u0)))
    qkv_xc.append(beside(gate(qkv_x[1], u0)))
    kept, sent = halved(kept + gate(arrived, u0).astype(F32), 2)
    next_input = lax.ppermute(gate(tokens_here, u0), "pipe", before)
    received = [sends(u0)]
    layers.append([[qkv_r[1]], [qkv_x[1]], [qkv_rc[1]], [qkv_xc[1]]])
    u1, table1 = project(1, qkv_xc[1], sent)
    rest = [ring_shifted(gate(qkv_x[2], u1)[:cut]), across(gate(qkv_r[3], u1)[cut:])]
    qkv_rc.append(beside(gate(qkv_r[3], u1)))
    qkv_xc.append(beside(gate(qkv_x[2], u1)))
    arrived = across(gate(sent, u1))
    next_cot = lax.ppermute(gate(cot, u1), "pipe", before)
    received.append(sends(u1))
    layers.append([[qkv_r[2]], [qkv_x[2]], [qkv_rc[2]], [qkv_xc[2]]])
    u2, table2 = project(2, qkv_xc[2], received[0], next_input)
    layers.append([[qkv_r[3]], rest, [qkv_rc[3]], [beside(gate(piece, u2)) for piece in rest]])
    received.append(sends(u2))
    u3, table3 = project(3, received[1], next_cot)
    kept, sent = halved(kept + gate(arrived, u2).astype(F32), 4)
    arrived = swapped(sent, 4)
    kept, sent = halved(kept + gate(arrived, u3).astype(F32), 8)
    arrived = swapped(sent, 8)
    received.append(sends(u3))

    tables = jnp.stack([table0, table1, table2, table3])
    order = (place[0] - jnp.arange(ring) + ring) % ring
    tables = jnp.take(tables, order, axis=0).transpose(1, 0, 2).reshape(2, width)
    table_part = jnp.concatenate([tables, gate_sum], axis=0)
    (passed_back,) = call(
        lambda *refs: finish_kernel(ring, *refs),
        [shape(rows, width)],
        "svv" + "v" * ring,
        [place, next_input, next_cot, *received],
        4,
        scratch=[pltpu.VMEM((rows, width), F32)],
        name="finish",
    )
    table_sum = exchanged_sum(table_part, passed_back)
    adapter_sum = (kept + gate(arrived, passed_back).astype(F32))[0]
    return (passed_back[None], (table_sum / count)[None], (adapter_sum / count)[None])


def solution(mesh):
    placed = (
        P("pipe", "dp", None),
        P("pipe", "dp", None),
        P("pipe", "dp", None),
        P("pipe", None, None),
        P("pipe", "dp", None),
        P("pipe", "dp"),
        P("pipe", "dp"),
        P("pipe", "dp", None),
        P("pipe", "dp", None),
        P("pipe", "dp", None),
        P("pipe", None, None),
    )
    return jax.shard_map(
        on_device,
        mesh=mesh,
        in_specs=placed,
        out_specs=(P("pipe", "dp", None), P("pipe", None, None), P("pipe", "dp", None)),
        check_vma=False,
    )
```

```python
import jax
import jax.numpy as jnp
from jax import lax
from jax.experimental import pallas as pl
from jax.experimental.pallas import tpu as pltpu
from jax.sharding import PartitionSpec as P

HEAD = 128
TILE = 128


EPSILON = 1e-06
HIGH = lax.Precision.HIGHEST


def contract_last(left, right):
    return lax.dot_general(
        left, right, (((1,), (1,)), ((), ())), preferred_element_type=jnp.float32
    )


def contract_first(left, right):
    return lax.dot_general(
        left, right, (((0,), (0,)), ((), ())), preferred_element_type=jnp.float32
    )


def swapped(block, bit):
    devices = range(lax.axis_size("dp"))
    return lax.ppermute(block, "dp", [(i, i ^ bit) for i in devices])


def ring_shifted(block):
    count = lax.axis_size("dp")
    return lax.ppermute(block, "dp", [(i, (i + 4) % count) for i in range(count)])


def lane_gather(block):
    me = lax.axis_index("dp")
    count = lax.axis_size("dp")
    rows, columns = block.shape
    whole = jnp.zeros((count // 2 * rows, columns), block.dtype)
    here = block
    for step in range(count // 4):
        if step:
            here = ring_shifted(here)
        across = swapped(here, 2)
        chip = (me - 4 * step + count) % count // 2
        whole = lax.dynamic_update_slice(whole, here, (chip * rows, 0))
        whole = lax.dynamic_update_slice(whole, across, ((chip ^ 1) * rows, 0))
    return whole


def interleaved(mine, other, lane, rows):
    first = jnp.where(lane == 0, mine, other)
    second = jnp.where(lane == 0, other, mine)
    columns = mine.shape[1]
    both = jnp.stack([first.reshape(-1, rows, columns), second.reshape(-1, rows, columns)], axis=1)
    return both.reshape(-1, columns)


def scatter_sum(part):
    me = lax.axis_index("dp")
    count = lax.axis_size("dp")
    rows, columns = part.shape
    kept = part.reshape(count, rows // count, columns)
    bit = 1
    while bit < count:
        mine = (me // bit) % 2
        pairs = kept.reshape(-1, 2, rows // count, columns)
        sent = lax.dynamic_index_in_dim(pairs, 1 - mine, 1, keepdims=False).astype(jnp.bfloat16)
        kept = lax.dynamic_index_in_dim(pairs, mine, 1, keepdims=False)
        kept = kept + swapped(sent, bit).astype(jnp.float32)
        bit *= 2
    return kept[0]


def whole_sum(part):
    bit = 1
    while bit < lax.axis_size("dp"):
        part = part + swapped(part, bit)
        bit *= 2
    return part


def on_device_general(
    block_input,
    saved_qkv,
    cotangent,
    mod_table,
    clip_condition,
    clip_frames,
    frame_tokens,
    tile_layout,
    frozen_qkv,
    frozen_out,
    adapters,
):
    lane = lax.axis_index("dp") % 2
    tokens_here = block_input[0]
    rows, width = tokens_here.shape
    saved = saved_qkv[0]
    inner = saved.shape[1] // 3
    heads = inner // HEAD
    slots = clip_frames.shape[1]
    tiles = tile_layout.shape[1]
    adapter_rows = adapters[0]
    down_qkv = adapter_rows[:width]
    up_qkv = adapter_rows[width : width + 3 * inner]
    down_out = adapter_rows[width + 3 * inner : width + 4 * inner]
    up_out = adapter_rows[width + 4 * inner :]

    lane_out = lane_gather(frozen_out[0])
    out_whole = interleaved(lane_out, swapped(lane_out, 1), lane, frozen_out.shape[1])
    lane_qkv = lane_gather(frozen_qkv[0])

    clip_ends = jnp.cumsum(clip_frames[0] * frame_tokens[0])
    position = jnp.arange(rows, dtype=jnp.int32)
    clip_of = jnp.sum((position[:, None] >= clip_ends[None, :]).astype(jnp.int32), axis=1)
    onehot_clip = (clip_of[:, None] == jnp.arange(slots, dtype=jnp.int32)[None, :]).astype(
        jnp.float32
    )
    modulation = mod_table[0].reshape(1, 3 * width) + jnp.dot(
        onehot_clip, clip_condition[0], precision=HIGH
    )
    shift_rows = modulation[:, :width]
    scale_rows = modulation[:, width : 2 * width]
    gate_rows = modulation[:, 2 * width :]
    inputs_f = tokens_here.astype(jnp.float32)
    centered = inputs_f - jnp.mean(inputs_f, axis=1, keepdims=True)
    inverse = lax.rsqrt(jnp.mean(centered * centered, axis=1, keepdims=True) + EPSILON)
    normed = centered * inverse
    modded = (normed * (1.0 + scale_rows) + shift_rows).astype(jnp.bfloat16)
    tile_onehot = (
        (position // TILE)[:, None] == jnp.arange(tiles, dtype=jnp.int32)[None, :]
    ).astype(jnp.float32)
    live_rows = jnp.dot(tile_onehot, tile_layout[0].astype(jnp.float32), precision=HIGH)
    live_pairs = jnp.dot(live_rows, tile_onehot.T, precision=HIGH) > 0.5
    allowed = live_pairs & (clip_of[:, None] == clip_of[None, :])
    queries = saved[:, :inner].reshape(rows, heads, HEAD)
    key_rows = saved[:, inner : 2 * inner].reshape(rows, heads, HEAD)
    value_rows = saved[:, 2 * inner :].reshape(rows, heads, HEAD)
    factor = HEAD ** (-0.5)
    scores = (
        jnp.einsum("qhd,khd->hqk", queries, key_rows, preferred_element_type=jnp.float32) * factor
    )
    scores = jnp.where(allowed[None], scores, -jnp.inf)
    probs = jax.nn.softmax(scores, axis=2)
    probs_b = probs.astype(jnp.bfloat16)
    attention = (
        jnp.einsum("hqk,khd->qhd", probs_b, value_rows, preferred_element_type=jnp.float32)
        .reshape(rows, inner)
        .astype(jnp.bfloat16)
    )
    low_out = jnp.dot(attention, down_out, preferred_element_type=jnp.float32).astype(jnp.bfloat16)
    cotangent_f = cotangent[0].astype(jnp.float32)
    gated = (gate_rows * cotangent_f).astype(jnp.bfloat16)
    low_grad_out = jnp.dot(gated, up_out, preferred_element_type=jnp.float32).astype(jnp.bfloat16)
    low_in = jnp.dot(modded, down_qkv, preferred_element_type=jnp.float32).astype(jnp.bfloat16)
    branch = jnp.dot(attention, out_whole, preferred_element_type=jnp.float32) + contract_last(
        low_out, up_out
    )
    grad_attention = (
        contract_last(gated, out_whole) + contract_last(low_grad_out, down_out)
    ).astype(jnp.bfloat16)
    grad_heads = grad_attention.reshape(rows, heads, HEAD)
    grad_probs = jnp.einsum(
        "qhd,khd->hqk", grad_heads, value_rows, preferred_element_type=jnp.float32
    )
    delta = jnp.sum(probs * grad_probs, axis=2, keepdims=True)
    grad_scores = (probs * (grad_probs - delta) * factor).astype(jnp.bfloat16)
    grad_query = jnp.einsum(
        "hqk,khd->qhd", grad_scores, key_rows, preferred_element_type=jnp.float32
    ).reshape(rows, inner)
    grad_key = jnp.einsum(
        "hqk,qhd->khd", grad_scores, queries, preferred_element_type=jnp.float32
    ).reshape(rows, inner)
    grad_value = jnp.einsum(
        "hqk,qhd->khd", probs_b, grad_heads, preferred_element_type=jnp.float32
    ).reshape(rows, inner)
    grad_qkv = jnp.concatenate([grad_query, grad_key, grad_value], axis=1).astype(jnp.bfloat16)
    grad_beside = swapped(grad_qkv, 1)
    low_grad_in = jnp.dot(grad_qkv, up_qkv, preferred_element_type=jnp.float32).astype(jnp.bfloat16)
    adapter_part = jnp.concatenate(
        [
            contract_first(modded, low_grad_in),
            contract_first(grad_qkv, low_in),
            contract_first(attention, low_grad_out),
            contract_first(gated, low_out),
        ],
        axis=0,
    )
    replicas = lax.axis_size("dp")
    adapter_sum = scatter_sum(adapter_part)

    part_rows = frozen_qkv.shape[1]
    frozen_beside = swapped(contract_last(grad_beside, lane_qkv), 1)
    frozen_mine = contract_last(grad_qkv, lane_qkv)
    first = jnp.where(lane == 0, frozen_mine, frozen_beside).reshape(rows, -1, part_rows)
    second = jnp.where(lane == 0, frozen_beside, frozen_mine).reshape(rows, -1, part_rows)
    frozen_part = jnp.stack([first, second], axis=2).reshape(rows, width)
    grad_modded = frozen_part + contract_last(low_grad_in, down_qkv)
    grad_normed = grad_modded * (1.0 + scale_rows)
    grad_input = cotangent_f + inverse * (
        grad_normed
        - jnp.mean(grad_normed, axis=1, keepdims=True)
        - normed * jnp.mean(grad_normed * normed, axis=1, keepdims=True)
    )
    grad_input = grad_input.astype(jnp.bfloat16)
    table_part = jnp.stack(
        [
            jnp.sum(grad_modded, axis=0),
            jnp.sum(grad_modded * normed, axis=0),
            jnp.sum(cotangent_f * branch, axis=0),
        ]
    )
    stages = lax.axis_size("pipe")
    passed_back = lax.ppermute(
        grad_input, "pipe", [((i + 1) % stages, i) for i in range(stages)]
    )
    table_sum = whole_sum(table_part)
    return (passed_back[None], (table_sum / replicas)[None], (adapter_sum / replicas)[None])


VMEM_LIMIT = 58 * 1024 * 1024
PACE = 1.0e6
F32 = jnp.float32
BF16 = jnp.bfloat16


def dot_nn(left, right):
    return lax.dot_general(
        left, right, (((1,), (0,)), ((), ())), preferred_element_type=jnp.float32
    )


def clip_numbers(frames_ref, sizes_ref, position):
    clip = jnp.zeros_like(position)
    end = jnp.int32(0)
    for slot in range(frames_ref.shape[1]):
        end = end + frames_ref[0, slot] * sizes_ref[0, slot]
        clip = clip + (position >= end).astype(jnp.int32)
    return clip


def mask_bias(frames_ref, sizes_ref, layout_ref, rows):
    down = lax.broadcasted_iota(jnp.int32, (rows, 1), 0)
    across = lax.broadcasted_iota(jnp.int32, (1, rows), 1)
    same = clip_numbers(frames_ref, sizes_ref, down) == clip_numbers(frames_ref, sizes_ref, across)
    live = jnp.zeros((rows, rows), jnp.int32)
    for i in range(rows // TILE):
        for j in range(rows // TILE):
            inside = (across // TILE == i) & (down // TILE == j)
            live = jnp.where(inside, layout_ref[0, i, j], live)
    return jnp.where(same & (live > 0), 0.0, -jnp.inf).astype(jnp.float32)


def pre_kernel(
    place_ref, frames_ref, sizes_ref, input_ref, cotangent_ref, table_ref, condition_ref, adapters_ref,
    modded_ref, gated_ref, normed_ref, scale_ref, low_in_ref, low_grad_ref,
    down_ref, up_ref, sems,
):
    rows, width = input_ref.shape
    slots = condition_ref.shape[0]
    down = pltpu.make_async_copy(adapters_ref.at[0, :width, :], down_ref, sems.at[0])
    up = pltpu.make_async_copy(adapters_ref.at[0, adapters_ref.shape[1] - width :, :], up_ref, sems.at[1])
    down.start()
    up.start()
    position = lax.broadcasted_iota(jnp.int32, (rows, 1), 0)
    clip = clip_numbers(frames_ref, sizes_ref, position)
    whole = condition_ref[...]
    high = whole.astype(BF16)
    rest = whole - high.astype(F32)
    middle = rest.astype(BF16)
    low = (rest - middle.astype(F32)).astype(BF16)
    parts = jnp.concatenate([high.astype(F32), middle.astype(F32), low.astype(F32)], axis=0)
    lanes = lax.broadcasted_iota(jnp.int32, (rows, 3 * slots), 1) % slots
    onehot = (clip == lanes).astype(F32).astype(BF16)
    parts = parts.astype(BF16)

    def modulation(which):
        columns = slice(which * width, (which + 1) * width)
        return dot_nn(onehot, parts[:, columns]) + table_ref[which : which + 1, :]

    inputs_f = input_ref[...].astype(F32)
    centered = inputs_f - jnp.mean(inputs_f, axis=1, keepdims=True)
    inverse = lax.rsqrt(jnp.mean(centered * centered, axis=1, keepdims=True) + EPSILON)
    normed = centered * inverse
    normed_ref[...] = normed
    scale = 1.0 + modulation(1)
    scale_ref[...] = scale
    modded = (normed * scale + modulation(0)).astype(BF16)
    modded_ref[...] = modded
    gated = (modulation(2) * cotangent_ref[...].astype(F32)).astype(BF16)
    gated_ref[...] = gated
    down.wait()
    low_in_ref[...] = dot_nn(modded, down_ref[...]).astype(BF16)
    up.wait()
    low_grad_ref[...] = dot_nn(gated, up_ref[...]).astype(BF16)


def forward_kernel(
    place_ref, frames_ref, sizes_ref, layout_ref, low_grad_ref, saved_in_ref, gated_in_ref,
    cotangent_in_ref, adapters_ref, attention_ref, low_out_ref, gate_ref, grad_down_ref, grad_up_ref,
    bias_ref, level_ref, down_ref, up_ref, saved_ref, gated_ref, cotangent_ref, sems,
):
    rows, inner = attention_ref.shape
    width = up_ref.shape[0]
    count = adapters_ref.shape[1]
    down = pltpu.make_async_copy(
        adapters_ref.at[0, count - width - inner : count - width, :], down_ref, sems.at[0]
    )
    up = pltpu.make_async_copy(adapters_ref.at[0, count - width :, :], up_ref, sems.at[1])
    factor = HEAD ** (-0.5)
    group = 3
    held = []
    for n, start in enumerate(range(0, inner, group * HEAD)):
        stop = min(start + group * HEAD, inner)
        for part in range(3):
            columns = slice(part * inner + start, part * inner + stop)
            held.append(
                pltpu.make_async_copy(
                    saved_in_ref.at[:, columns], saved_ref.at[:, columns], sems.at[4 + 3 * n + part]
                )
            )
    gated_copy = pltpu.make_async_copy(gated_in_ref, gated_ref, sems.at[2])
    cotangent_copy = pltpu.make_async_copy(cotangent_in_ref, cotangent_ref, sems.at[3])
    for copy in held + [down, gated_copy, cotangent_copy, up]:
        copy.start()
    bias_ref[...] = mask_bias(frames_ref, sizes_ref, layout_ref, rows)
    for start in range(0, inner // HEAD, group):
        heads = range(start, min(start + group, inner // HEAD))
        for copy in held[start // group * 3 : start // group * 3 + 3]:
            copy.wait()
        scores = []
        for head in heads:
            query = saved_ref[:, head * HEAD : (head + 1) * HEAD]
            key = saved_ref[:, inner + head * HEAD : inner + (head + 1) * HEAD]
            scores.append(contract_last(key, query) * factor + bias_ref[...])
        probs = []
        for head, score in zip(heads, scores):
            most = jnp.max(score, axis=0, keepdims=True)
            raised = jnp.exp(score - most)
            whole = jnp.sum(raised, axis=0, keepdims=True)
            level_ref[head : head + 1, :] = most + jnp.log(whole)
            probs.append((raised * (1.0 / whole)).astype(BF16))
        for head, prob in zip(heads, probs):
            value = saved_ref[:, 2 * inner + head * HEAD : 2 * inner + (head + 1) * HEAD]
            attention_ref[:, head * HEAD : (head + 1) * HEAD] = contract_first(prob, value).astype(BF16)
    down.wait()
    attention = attention_ref[...]
    low_out = dot_nn(attention, down_ref[...]).astype(BF16)
    low_out_ref[...] = low_out
    grad_down_ref[...] = contract_first(attention, low_grad_ref[...])
    gated_copy.wait()
    grad_up_ref[...] = contract_first(gated_ref[...], low_out)
    up.wait()
    cotangent_copy.wait()
    branch = contract_last(low_out, up_ref[...])
    gate_ref[...] = jnp.sum(branch * cotangent_ref[...].astype(F32), axis=0, keepdims=True)


def layer_of(place_ref, step):
    ring = place_ref[2]
    return lax.rem(place_ref[0] - step + ring, ring)


def shard_copies(place_ref, shards, whole_ref, sems):
    copies = []
    for pieces, flip in zip(shards, (0, 2, 1, 3)):
        owner = (place_ref[1] ^ flip) * (whole_ref.shape[0] // 4)
        offset = 0
        for piece in pieces:
            start = pl.multiple_of(owner + offset, 16)
            offset += piece.shape[0]
            target = whole_ref.at[pl.ds(start, piece.shape[0]), :]
            copies.append(pltpu.make_async_copy(piece, target, sems.at[len(copies)]))
    return copies


def nested(refs, sizes):
    refs = list(refs)
    return [[refs.pop(0) for _ in range(size)] for size in sizes]


def backward_kernel(
    step, sizes,
    place_ref, low_grad_ref, low_in_ref, bias_ref, level_ref, gate_in_ref, total_in_ref,
    gated_in_ref, cotangent_in_ref, saved_ref, attention_ref, adapters_ref, *refs,
):
    shards = nested(refs, sizes)
    refs = refs[sum(sizes) :]
    grad_ref, grad_up_ref, gate_ref, total_ref = refs[:4]
    whole_ref, held_ref, out_ref, down_ref, up_ref, gated_ref, cotangent_ref, sems = refs[4:]
    depth, width = whole_ref.shape
    inner = attention_ref.shape[1]
    first = pl.multiple_of(layer_of(place_ref, step) * depth, HEAD)
    layer = pl.ds(first, depth)
    weights = shard_copies(place_ref, shards, whole_ref, sems)
    used = len(weights)
    parts = [pl.ds(pl.multiple_of(part * inner + first, HEAD), depth) for part in range(3)]
    held = [
        pltpu.make_async_copy(saved_ref.at[:, parts[part]], held_ref.at[part], sems.at[used + part])
        for part in range(3)
    ]
    others = [
        pltpu.make_async_copy(gated_in_ref, gated_ref, sems.at[used + 8]),
        pltpu.make_async_copy(cotangent_in_ref, cotangent_ref, sems.at[used + 9]),
        pltpu.make_async_copy(attention_ref.at[:, layer], out_ref, sems.at[used + 3]),
        pltpu.make_async_copy(
            adapters_ref.at[0, pl.ds(pl.multiple_of(width + 3 * inner + first, HEAD), depth), :],
            down_ref,
            sems.at[used + 4],
        ),
    ] + [
        pltpu.make_async_copy(
            adapters_ref.at[0, pl.ds(pl.multiple_of(width + part * inner + first, HEAD), depth), :],
            up_ref.at[pl.ds(part * depth, depth), :],
            sems.at[used + 5 + part],
        )
        for part in range(3)
    ]
    for copy in held + weights + others:
        copy.start()
    factor = HEAD ** (-0.5)
    heads = range(depth // HEAD)
    spans = [slice(head * HEAD, (head + 1) * HEAD) for head in heads]
    for copy in held:
        copy.wait()
    probs = []
    for head in heads:
        scores = contract_last(held_ref[1, :, spans[head]], held_ref[0, :, spans[head]]) * factor
        level = level_ref[pl.ds(layer_of(place_ref, step) * len(heads) + head, 1), :]
        probs.append(jnp.exp(scores + (bias_ref[...] - level)))
    for copy in weights + others:
        copy.wait()
    grad_attention = (
        contract_last(gated_ref[...], whole_ref[...])
        + contract_last(low_grad_ref[...], down_ref[...])
    ).astype(BF16)
    grad_scores = []
    for head in heads:
        grad = grad_attention[:, spans[head]]
        grad_probs = contract_last(held_ref[2, :, spans[head]], grad)
        delta = jnp.sum(probs[head] * grad_probs, axis=0, keepdims=True)
        grad_scores.append((probs[head] * ((grad_probs - delta) * factor)).astype(BF16))
    for head in heads:
        grad = grad_attention[:, spans[head]]
        pieces = (
            contract_first(grad_scores[head], held_ref[1, :, spans[head]]),
            dot_nn(grad_scores[head], held_ref[0, :, spans[head]]),
            dot_nn(probs[head].astype(BF16), grad),
        )
        for part, piece in enumerate(pieces):
            columns = slice(part * depth + head * HEAD, part * depth + (head + 1) * HEAD)
            grad_ref[:, columns] = piece.astype(BF16)
    grads = grad_ref[...]
    grad_up_ref[...] = contract_first(grads, low_in_ref[...])
    total_ref[...] = total_in_ref[...] + dot_nn(grads, up_ref[...])
    branch = dot_nn(out_ref[...], whole_ref[...])
    gate_ref[...] = gate_in_ref[...] + jnp.sum(
        branch * cotangent_ref[...].astype(F32), axis=0, keepdims=True
    )


def adapter_kernel(
    ring, place_ref, modded_ref, total_ref, grad_down_ref, grad_up_ref, *refs,
):
    layer_refs, (low_ref, sent_ref, kept_ref, whole_ref) = refs[:ring], refs[ring:]
    width = modded_ref.shape[1]
    inner = grad_down_ref.shape[0]
    depth = inner // ring
    low = total_ref[...].astype(BF16)
    low_ref[...] = low
    whole_ref[:width, :] = contract_first(modded_ref[...], low)
    for step in range(ring):
        first = layer_of(place_ref, step) * depth
        for part in range(3):
            start = pl.multiple_of(width + part * inner + first, HEAD)
            whole_ref[pl.ds(start, depth), :] = layer_refs[step][part * depth : (part + 1) * depth, :]
    whole_ref[width + 3 * inner : width + 4 * inner, :] = grad_down_ref[...]
    whole_ref[width + 4 * inner :, :] = grad_up_ref[...]
    blocks, block = kept_ref.shape[0], kept_ref.shape[1]
    lane = place_ref[1] % 2
    for j in range(blocks):
        mine = pl.multiple_of((2 * j + lane) * block, 64)
        other = pl.multiple_of((2 * j + 1 - lane) * block, 64)
        kept_ref[j] = whole_ref[pl.ds(mine, block), :]
        sent_ref[j] = whole_ref[pl.ds(other, block), :].astype(BF16)


def input_kernel(
    step, ring, sizes, place_ref, low_ref, table_in_ref, *refs,
):
    grad_refs, refs = refs[:ring], refs[ring:]
    normed_ref, scale_ref, adapters_ref = refs[:3]
    shards = nested(refs[3:], sizes)
    u_ref, table_ref, whole_ref, near_ref, down_ref, held_ref, sems = refs[3 + sum(sizes) :]
    depth = whole_ref.shape[0]
    inner = whole_ref.shape[1] // 3
    weights = shard_copies(place_ref, shards, whole_ref, sems)
    used = len(weights)
    first = pl.multiple_of(layer_of(place_ref, step) * depth, HEAD)
    layer = pl.ds(first, depth)
    others = [
        pltpu.make_async_copy(adapters_ref.at[0, layer, :], down_ref, sems.at[used]),
        pltpu.make_async_copy(normed_ref.at[:, layer], near_ref.at[0], sems.at[used + 1]),
        pltpu.make_async_copy(scale_ref.at[:, layer], near_ref.at[1], sems.at[used + 2]),
    ]
    for n in range(ring):
        start = layer_of(place_ref, n) * depth
        for part in range(3):
            columns = pl.ds(pl.multiple_of(part * inner + start, HEAD), depth)
            others.append(
                pltpu.make_async_copy(
                    grad_refs[n].at[:, part * depth : (part + 1) * depth],
                    held_ref.at[:, columns],
                    sems.at[used + 3 + 3 * n + part],
                )
            )
    for copy in weights + others:
        copy.start()
    for copy in weights + others:
        copy.wait()
    total = contract_last(held_ref[...], whole_ref[...])
    total = total + contract_last(low_ref[...], down_ref[...])
    u_ref[...] = (total * near_ref[1]).astype(BF16)
    table_ref[...] = table_in_ref[...]
    table_ref[0:1, layer] = jnp.sum(total, axis=0, keepdims=True)
    table_ref[1:2, layer] = jnp.sum(total * near_ref[0], axis=0, keepdims=True)


def finish_kernel(ring, place_ref, input_ref, cotangent_ref, *refs):
    u_refs, (out_ref, u_ref) = refs[:ring], refs[ring:]
    depth = u_refs[0].shape[1]
    for step in range(ring):
        layer = pl.ds(pl.multiple_of(layer_of(place_ref, step) * depth, HEAD), depth)
        u_ref[:, layer] = u_refs[step][...].astype(F32)
    inputs_f = input_ref[...].astype(F32)
    centered = inputs_f - jnp.mean(inputs_f, axis=1, keepdims=True)
    inverse = lax.rsqrt(jnp.mean(centered * centered, axis=1, keepdims=True) + EPSILON)
    normed = centered * inverse
    u = u_ref[...]
    out_ref[...] = (
        cotangent_ref[...].astype(F32)
        + inverse
        * (
            u
            - jnp.mean(u, axis=1, keepdims=True)
            - normed * jnp.mean(u * normed, axis=1, keepdims=True)
        )
    ).astype(BF16)


def call(kernel, outs, specs, operands, time, scratch=(), name=None):
    space = {"s": pltpu.SMEM, "v": pltpu.VMEM, "a": pl.ANY}
    return pl.pallas_call(
        kernel,
        out_shape=outs,
        in_specs=[pl.BlockSpec(memory_space=space[s]) for s in specs],
        out_specs=[pl.BlockSpec(memory_space=pltpu.VMEM)] * len(outs),
        scratch_shapes=list(scratch),
        compiler_params=pltpu.CompilerParams(vmem_limit_bytes=VMEM_LIMIT),
        cost_estimate=pl.CostEstimate(flops=0, bytes_accessed=int(time * PACE), transcendentals=0),
        name=name,
    )(*operands)


def shape(*dims, dtype=BF16):
    return jax.ShapeDtypeStruct(dims, dtype)


def gate(value, *events):
    return lax.optimization_barrier((value, *events))[0]


def exchanged_sum(part, event):
    count = lax.axis_size("dp")
    total = part
    for flip in (1, 2, 3):
        total = total + swapped(part, flip)
    part = total
    for distance in range(4, count, 4):
        route = [(i, (i + distance) % count) for i in range(count)]
        total = total + gate(lax.ppermute(part, "dp", route), event)
    return total


def on_device(
    block_input,
    saved_qkv,
    cotangent,
    mod_table,
    clip_condition,
    clip_frames,
    frame_tokens,
    tile_layout,
    frozen_qkv,
    frozen_out,
    adapters,
):
    count = lax.axis_size("dp")
    depth = 4 * frozen_out.shape[1]
    if count != 16 or depth % HEAD or depth != 4 * frozen_qkv.shape[1]:
        return on_device_general(
            block_input, saved_qkv, cotangent, mod_table, clip_condition, clip_frames,
            frame_tokens, tile_layout, frozen_qkv, frozen_out, adapters,
        )
    ring = count // 4
    me = lax.axis_index("dp")
    place = jnp.stack([me // 4, me % 4, jnp.int32(ring)]).astype(jnp.int32)
    tokens_here, saved, cot = block_input[0], saved_qkv[0], cotangent[0]
    rows, width = tokens_here.shape
    inner = saved.shape[1] // 3
    rank = adapters.shape[2]
    heads = inner // HEAD
    stages = lax.axis_size("pipe")
    before = [((i + 1) % stages, i) for i in range(stages)]
    clips = [clip_frames, frame_tokens]
    beside = lambda block: swapped(block, 1)
    across = lambda block: swapped(block, 2)

    out_r, qkv_r = [frozen_out[0]], [frozen_qkv[0]]
    out_r.append(ring_shifted(out_r[0]))
    out_x = [across(out_r[0])]
    out_rc, out_xc, qkv_x, qkv_rc, qkv_xc = [beside(out_r[0])], [], [], [], []
    modded, gated, normed, scale, low_in, low_grad_out = call(
        pre_kernel,
        [shape(rows, width), shape(rows, width), shape(rows, width, dtype=F32),
         shape(rows, width, dtype=F32), shape(rows, rank), shape(rows, rank)],
        "sssvvvva",
        [place, *clips, tokens_here, cot, mod_table[0], clip_condition[0], adapters],
        4,
        scratch=[pltpu.VMEM((width, rank), BF16), pltpu.VMEM((width, rank), BF16), pltpu.SemaphoreType.DMA((2,))],
        name="modulate",
    )
    event = low_in
    next_input = lax.ppermute(gate(tokens_here, event), "pipe", before)
    out_r.append(ring_shifted(gate(out_r[1], event)))
    out_x.append(across(gate(out_r[1], event)))
    out_xc.append(beside(gate(out_x[0], event)))
    attention, low_out, gate_sum, grad_down_out, grad_up_out, bias, level = call(
        forward_kernel,
        [shape(rows, inner), shape(rows, rank), shape(1, width, dtype=F32),
         shape(inner, rank, dtype=F32), shape(width, rank, dtype=F32),
         shape(rows, rows, dtype=F32), shape(heads, rows, dtype=F32)],
        "ssssvaaaa",
        [gate(place, out_r[1], out_x[0]), *clips, tile_layout, low_grad_out, saved, gated, cot, adapters],
        6,
        scratch=[
            pltpu.VMEM((inner, rank), BF16), pltpu.VMEM((width, rank), BF16),
            pltpu.VMEM(saved.shape, BF16), pltpu.VMEM((rows, width), BF16),
            pltpu.VMEM((rows, width), BF16), pltpu.SemaphoreType.DMA((4 + 3 * heads,)),
        ],
        name="attend",
    )

    event = low_out

    def backward(step, gate_sum, total, *waited):
        shards = ([out_r[step]], [out_x[step]], [out_rc[step]], [out_xc[step]])
        return call(
            lambda *refs: backward_kernel(step, [1, 1, 1, 1], *refs),
            [shape(rows, 3 * depth), shape(3 * depth, rank, dtype=F32),
             shape(1, width, dtype=F32), shape(rows, rank, dtype=F32)],
            "svvvvvvaaaaaaaaa",
            [gate(place, *waited), low_grad_out, low_in, bias, level, gate_sum, total, gated, cot, saved,
             attention, adapters, *sum(shards, [])],
            5,
            scratch=[
                pltpu.VMEM((depth, width), BF16), pltpu.VMEM((3, rows, depth), BF16),
                pltpu.VMEM((rows, depth), BF16), pltpu.VMEM((depth, rank), BF16),
                pltpu.VMEM((3 * depth, rank), BF16), pltpu.VMEM((rows, width), BF16),
                pltpu.VMEM((rows, width), BF16), pltpu.SemaphoreType.DMA((14,)),
            ],
            name=f"backward{step}",
        )

    total = jnp.zeros((rows, rank), F32)
    out_r.append(ring_shifted(gate(out_r[2], event)))
    out_x.append(across(gate(out_r[2], event)))
    out_rc.append(beside(gate(out_r[1], event)))
    out_xc.append(beside(gate(out_x[1], event)))
    grad0, grad_up0, gate_sum, total = backward(0, gate_sum, total, out_r[2], out_x[1], out_xc[0])
    event = total
    out_x.append(across(gate(out_r[3], event)))
    qkv_r.append(ring_shifted(gate(qkv_r[0], event, out_r[3])))
    qkv_rc.append(beside(gate(qkv_r[0], event)))
    out_rc.append(beside(gate(out_r[2], event)))
    out_xc.append(beside(gate(out_x[2], event)))
    grad1, grad_up1, gate_sum, total = backward(1, gate_sum, total, out_r[3], out_x[2])
    event = total
    qkv_x.append(across(gate(qkv_r[0], event, out_x[3])))
    next_cot = lax.ppermute(gate(cot, event), "pipe", before)
    out_rc.append(beside(gate(out_r[3], event)))
    out_xc.append(beside(gate(out_x[3], event)))
    grad2, grad_up2, gate_sum, total = backward(2, gate_sum, total, out_x[3])
    grad3, grad_up3, gate_sum, total = backward(3, gate_sum, total, next_input)
    event = total
    grads = [grad0, grad1, grad2, grad3]
    grad_ups = [grad_up0, grad_up1, grad_up2, grad_up3]

    block = adapters.shape[1] // count
    low_grad_in, sent, kept = call(
        lambda *refs: adapter_kernel(ring, *refs),
        [shape(rows, rank), shape(count // 2, block, rank), shape(count // 2, block, rank, dtype=F32)],
        "svvvv" + "v" * ring,
        [place, modded, total, grad_down_out, grad_up_out, *grad_ups],
        4,
        scratch=[pltpu.VMEM(adapters.shape[1:], F32)],
        name="adapt",
    )

    def project(step, *waited):
        shards = layers[step]
        sizes = [len(shard) for shard in shards]
        return call(
            lambda *refs: input_kernel(step, ring, sizes, *refs),
            [shape(rows, depth), shape(3, width, dtype=F32)],
            "svv" + "a" * ring + "aaa" + "a" * sum(sizes),
            [gate(place, *waited), low_grad_in, table, *grads, normed, scale, adapters, *sum(shards, [])],
            5,
            scratch=[
                pltpu.VMEM((depth, 3 * inner), BF16), pltpu.VMEM((2, rows, depth), F32),
                pltpu.VMEM((depth, rank), BF16), pltpu.VMEM((rows, 3 * inner), BF16),
                pltpu.SemaphoreType.DMA((9 + 3 * ring,)),
            ],
            name=f"project{step}",
        )

    def halved(kept, bit):
        mine = (me // bit) % 2
        pairs = kept.reshape(-1, 2, block, rank)
        sent = lax.dynamic_index_in_dim(pairs, 1 - mine, 1, keepdims=False).astype(BF16)
        return lax.dynamic_index_in_dim(pairs, mine, 1, keepdims=False), sent

    sends = lambda u: lax.ppermute(u, "pipe", before)
    event = low_grad_in
    qkv_r.append(ring_shifted(gate(qkv_r[1], event)))
    qkv_x.append(across(gate(qkv_r[1], event)))
    qkv_rc.append(beside(gate(qkv_r[1], event)))
    qkv_xc.append(beside(gate(qkv_x[0], event)))
    arrived = beside(sent)
    layers = [[[qkv_r[0]], [qkv_x[0]], [qkv_rc[0]], [qkv_xc[0]]]]
    table = jnp.concatenate([jnp.zeros((2, width), F32), gate_sum], axis=0)
    u0, table = project(0, qkv_xc[0], next_cot)
    qkv_r.append(ring_shifted(gate(qkv_r[2], u0)))
    qkv_x.append(across(gate(qkv_r[2], u0)))
    qkv_rc.append(beside(gate(qkv_r[2], u0)))
    qkv_xc.append(beside(gate(qkv_x[1], u0)))
    kept, sent = halved(kept + gate(arrived, u0).astype(F32), 2)
    received = [sends(u0)]
    layers.append([[qkv_r[1]], [qkv_x[1]], [qkv_rc[1]], [qkv_xc[1]]])
    u1, table = project(1, qkv_xc[1], sent, received[0])
    rest = [ring_shifted(gate(qkv_x[2], u1))]
    qkv_rc.append(beside(gate(qkv_r[3], u1)))
    qkv_xc.append(beside(gate(qkv_x[2], u1)))
    arrived = across(gate(sent, u1))
    received.append(sends(u1))
    layers.append([[qkv_r[2]], [qkv_x[2]], [qkv_rc[2]], [qkv_xc[2]]])
    u2, table = project(2, qkv_xc[2], received[1])
    layers.append([[qkv_r[3]], rest, [qkv_rc[3]], [beside(gate(piece, u2)) for piece in rest]])
    received.append(sends(u2))
    u3, table = project(3)
    kept, sent = halved(kept + gate(arrived, u2).astype(F32), 4)
    arrived = swapped(sent, 4)
    kept, sent = halved(kept + gate(arrived, u3).astype(F32), 8)
    arrived = swapped(sent, 8)
    received.append(sends(u3))

    (passed_back,) = call(
        lambda *refs: finish_kernel(ring, *refs),
        [shape(rows, width)],
        "svv" + "v" * ring,
        [place, next_input, next_cot, *received],
        4,
        scratch=[pltpu.VMEM((rows, width), F32)],
        name="finish",
    )
    table_sum = exchanged_sum(table, passed_back)
    adapter_sum = (kept + gate(arrived, passed_back).astype(F32))[0]
    return (passed_back[None], (table_sum / count)[None], (adapter_sum / count)[None])


def solution(mesh):
    placed = (
        P("pipe", "dp", None),
        P("pipe", "dp", None),
        P("pipe", "dp", None),
        P("pipe", None, None),
        P("pipe", "dp", None),
        P("pipe", "dp"),
        P("pipe", "dp"),
        P("pipe", "dp", None),
        P("pipe", "dp", None),
        P("pipe", "dp", None),
        P("pipe", None, None),
    )
    return jax.shard_map(
        on_device,
        mesh=mesh,
        in_specs=placed,
        out_specs=(P("pipe", "dp", None), P("pipe", None, None), P("pipe", "dp", None)),
        check_vma=False,
    )
```

```python
import jax
import jax.numpy as jnp
from jax import lax
from jax.experimental import pallas as pl
from jax.experimental.pallas import tpu as pltpu
from jax.sharding import PartitionSpec as P

HEAD = 128
TILE = 128


EPSILON = 1e-06
HIGH = lax.Precision.HIGHEST


def contract_last(left, right):
    return lax.dot_general(
        left, right, (((1,), (1,)), ((), ())), preferred_element_type=jnp.float32
    )


def contract_first(left, right):
    return lax.dot_general(
        left, right, (((0,), (0,)), ((), ())), preferred_element_type=jnp.float32
    )


def swapped(block, bit):
    devices = range(lax.axis_size("dp"))
    return lax.ppermute(block, "dp", [(i, i ^ bit) for i in devices])


def ring_shifted(block):
    count = lax.axis_size("dp")
    return lax.ppermute(block, "dp", [(i, (i + 4) % count) for i in range(count)])


def lane_gather(block):
    me = lax.axis_index("dp")
    count = lax.axis_size("dp")
    rows, columns = block.shape
    whole = jnp.zeros((count // 2 * rows, columns), block.dtype)
    here = block
    for step in range(count // 4):
        if step:
            here = ring_shifted(here)
        across = swapped(here, 2)
        chip = (me - 4 * step + count) % count // 2
        whole = lax.dynamic_update_slice(whole, here, (chip * rows, 0))
        whole = lax.dynamic_update_slice(whole, across, ((chip ^ 1) * rows, 0))
    return whole


def interleaved(mine, other, lane, rows):
    first = jnp.where(lane == 0, mine, other)
    second = jnp.where(lane == 0, other, mine)
    columns = mine.shape[1]
    both = jnp.stack([first.reshape(-1, rows, columns), second.reshape(-1, rows, columns)], axis=1)
    return both.reshape(-1, columns)


def scatter_sum(part):
    me = lax.axis_index("dp")
    count = lax.axis_size("dp")
    rows, columns = part.shape
    kept = part.reshape(count, rows // count, columns)
    bit = 1
    while bit < count:
        mine = (me // bit) % 2
        pairs = kept.reshape(-1, 2, rows // count, columns)
        sent = lax.dynamic_index_in_dim(pairs, 1 - mine, 1, keepdims=False).astype(jnp.bfloat16)
        kept = lax.dynamic_index_in_dim(pairs, mine, 1, keepdims=False)
        kept = kept + swapped(sent, bit).astype(jnp.float32)
        bit *= 2
    return kept[0]


def whole_sum(part):
    bit = 1
    while bit < lax.axis_size("dp"):
        part = part + swapped(part, bit)
        bit *= 2
    return part


def on_device_general(
    block_input,
    saved_qkv,
    cotangent,
    mod_table,
    clip_condition,
    clip_frames,
    frame_tokens,
    tile_layout,
    frozen_qkv,
    frozen_out,
    adapters,
):
    lane = lax.axis_index("dp") % 2
    tokens_here = block_input[0]
    rows, width = tokens_here.shape
    saved = saved_qkv[0]
    inner = saved.shape[1] // 3
    heads = inner // HEAD
    slots = clip_frames.shape[1]
    tiles = tile_layout.shape[1]
    adapter_rows = adapters[0]
    down_qkv = adapter_rows[:width]
    up_qkv = adapter_rows[width : width + 3 * inner]
    down_out = adapter_rows[width + 3 * inner : width + 4 * inner]
    up_out = adapter_rows[width + 4 * inner :]

    lane_out = lane_gather(frozen_out[0])
    out_whole = interleaved(lane_out, swapped(lane_out, 1), lane, frozen_out.shape[1])
    lane_qkv = lane_gather(frozen_qkv[0])

    clip_ends = jnp.cumsum(clip_frames[0] * frame_tokens[0])
    position = jnp.arange(rows, dtype=jnp.int32)
    clip_of = jnp.sum((position[:, None] >= clip_ends[None, :]).astype(jnp.int32), axis=1)
    onehot_clip = (clip_of[:, None] == jnp.arange(slots, dtype=jnp.int32)[None, :]).astype(
        jnp.float32
    )
    modulation = mod_table[0].reshape(1, 3 * width) + jnp.dot(
        onehot_clip, clip_condition[0], precision=HIGH
    )
    shift_rows = modulation[:, :width]
    scale_rows = modulation[:, width : 2 * width]
    gate_rows = modulation[:, 2 * width :]
    inputs_f = tokens_here.astype(jnp.float32)
    centered = inputs_f - jnp.mean(inputs_f, axis=1, keepdims=True)
    inverse = lax.rsqrt(jnp.mean(centered * centered, axis=1, keepdims=True) + EPSILON)
    normed = centered * inverse
    modded = (normed * (1.0 + scale_rows) + shift_rows).astype(jnp.bfloat16)
    tile_onehot = (
        (position // TILE)[:, None] == jnp.arange(tiles, dtype=jnp.int32)[None, :]
    ).astype(jnp.float32)
    live_rows = jnp.dot(tile_onehot, tile_layout[0].astype(jnp.float32), precision=HIGH)
    live_pairs = jnp.dot(live_rows, tile_onehot.T, precision=HIGH) > 0.5
    allowed = live_pairs & (clip_of[:, None] == clip_of[None, :])
    queries = saved[:, :inner].reshape(rows, heads, HEAD)
    key_rows = saved[:, inner : 2 * inner].reshape(rows, heads, HEAD)
    value_rows = saved[:, 2 * inner :].reshape(rows, heads, HEAD)
    factor = HEAD ** (-0.5)
    scores = (
        jnp.einsum("qhd,khd->hqk", queries, key_rows, preferred_element_type=jnp.float32) * factor
    )
    scores = jnp.where(allowed[None], scores, -jnp.inf)
    probs = jax.nn.softmax(scores, axis=2)
    probs_b = probs.astype(jnp.bfloat16)
    attention = (
        jnp.einsum("hqk,khd->qhd", probs_b, value_rows, preferred_element_type=jnp.float32)
        .reshape(rows, inner)
        .astype(jnp.bfloat16)
    )
    low_out = jnp.dot(attention, down_out, preferred_element_type=jnp.float32).astype(jnp.bfloat16)
    cotangent_f = cotangent[0].astype(jnp.float32)
    gated = (gate_rows * cotangent_f).astype(jnp.bfloat16)
    low_grad_out = jnp.dot(gated, up_out, preferred_element_type=jnp.float32).astype(jnp.bfloat16)
    low_in = jnp.dot(modded, down_qkv, preferred_element_type=jnp.float32).astype(jnp.bfloat16)
    branch = jnp.dot(attention, out_whole, preferred_element_type=jnp.float32) + contract_last(
        low_out, up_out
    )
    grad_attention = (
        contract_last(gated, out_whole) + contract_last(low_grad_out, down_out)
    ).astype(jnp.bfloat16)
    grad_heads = grad_attention.reshape(rows, heads, HEAD)
    grad_probs = jnp.einsum(
        "qhd,khd->hqk", grad_heads, value_rows, preferred_element_type=jnp.float32
    )
    delta = jnp.sum(probs * grad_probs, axis=2, keepdims=True)
    grad_scores = (probs * (grad_probs - delta) * factor).astype(jnp.bfloat16)
    grad_query = jnp.einsum(
        "hqk,khd->qhd", grad_scores, key_rows, preferred_element_type=jnp.float32
    ).reshape(rows, inner)
    grad_key = jnp.einsum(
        "hqk,qhd->khd", grad_scores, queries, preferred_element_type=jnp.float32
    ).reshape(rows, inner)
    grad_value = jnp.einsum(
        "hqk,qhd->khd", probs_b, grad_heads, preferred_element_type=jnp.float32
    ).reshape(rows, inner)
    grad_qkv = jnp.concatenate([grad_query, grad_key, grad_value], axis=1).astype(jnp.bfloat16)
    grad_beside = swapped(grad_qkv, 1)
    low_grad_in = jnp.dot(grad_qkv, up_qkv, preferred_element_type=jnp.float32).astype(jnp.bfloat16)
    adapter_part = jnp.concatenate(
        [
            contract_first(modded, low_grad_in),
            contract_first(grad_qkv, low_in),
            contract_first(attention, low_grad_out),
            contract_first(gated, low_out),
        ],
        axis=0,
    )
    replicas = lax.axis_size("dp")
    adapter_sum = scatter_sum(adapter_part)

    part_rows = frozen_qkv.shape[1]
    frozen_beside = swapped(contract_last(grad_beside, lane_qkv), 1)
    frozen_mine = contract_last(grad_qkv, lane_qkv)
    first = jnp.where(lane == 0, frozen_mine, frozen_beside).reshape(rows, -1, part_rows)
    second = jnp.where(lane == 0, frozen_beside, frozen_mine).reshape(rows, -1, part_rows)
    frozen_part = jnp.stack([first, second], axis=2).reshape(rows, width)
    grad_modded = frozen_part + contract_last(low_grad_in, down_qkv)
    grad_normed = grad_modded * (1.0 + scale_rows)
    grad_input = cotangent_f + inverse * (
        grad_normed
        - jnp.mean(grad_normed, axis=1, keepdims=True)
        - normed * jnp.mean(grad_normed * normed, axis=1, keepdims=True)
    )
    grad_input = grad_input.astype(jnp.bfloat16)
    table_part = jnp.stack(
        [
            jnp.sum(grad_modded, axis=0),
            jnp.sum(grad_modded * normed, axis=0),
            jnp.sum(cotangent_f * branch, axis=0),
        ]
    )
    stages = lax.axis_size("pipe")
    passed_back = lax.ppermute(
        grad_input, "pipe", [((i + 1) % stages, i) for i in range(stages)]
    )
    table_sum = whole_sum(table_part)
    return (passed_back[None], (table_sum / replicas)[None], (adapter_sum / replicas)[None])


VMEM_LIMIT = 58 * 1024 * 1024
PACE = 1.0e6
F32 = jnp.float32
BF16 = jnp.bfloat16


def dot_nn(left, right):
    return lax.dot_general(
        left, right, (((1,), (0,)), ((), ())), preferred_element_type=jnp.float32
    )


def clip_numbers(frames_ref, sizes_ref, position):
    clip = jnp.zeros_like(position)
    end = jnp.int32(0)
    for slot in range(frames_ref.shape[1]):
        end = end + frames_ref[0, slot] * sizes_ref[0, slot]
        clip = clip + (position >= end).astype(jnp.int32)
    return clip


def mask_bias(frames_ref, sizes_ref, layout_ref, rows):
    down = lax.broadcasted_iota(jnp.int32, (rows, 1), 0)
    across = lax.broadcasted_iota(jnp.int32, (1, rows), 1)
    same = clip_numbers(frames_ref, sizes_ref, down) == clip_numbers(frames_ref, sizes_ref, across)
    live = jnp.zeros((rows, rows), jnp.int32)
    for i in range(rows // TILE):
        for j in range(rows // TILE):
            inside = (across // TILE == i) & (down // TILE == j)
            live = jnp.where(inside, layout_ref[0, i, j], live)
    return jnp.where(same & (live > 0), 0.0, -jnp.inf).astype(jnp.float32)


def pre_kernel(
    place_ref, frames_ref, sizes_ref, input_ref, cotangent_ref, table_ref, condition_ref, adapters_ref,
    modded_ref, gated_ref, normed_ref, scale_ref, low_in_ref, low_grad_ref,
    down_ref, up_ref, sems,
):
    rows, width = input_ref.shape
    slots = condition_ref.shape[0]
    down = pltpu.make_async_copy(adapters_ref.at[0, :width, :], down_ref, sems.at[0])
    up = pltpu.make_async_copy(adapters_ref.at[0, adapters_ref.shape[1] - width :, :], up_ref, sems.at[1])
    down.start()
    up.start()
    position = lax.broadcasted_iota(jnp.int32, (rows, 1), 0)
    clip = clip_numbers(frames_ref, sizes_ref, position)
    whole = condition_ref[...]
    high = whole.astype(BF16)
    rest = whole - high.astype(F32)
    middle = rest.astype(BF16)
    low = (rest - middle.astype(F32)).astype(BF16)
    parts = jnp.concatenate([high.astype(F32), middle.astype(F32), low.astype(F32)], axis=0)
    lanes = lax.broadcasted_iota(jnp.int32, (rows, 3 * slots), 1) % slots
    onehot = (clip == lanes).astype(F32).astype(BF16)
    parts = parts.astype(BF16)

    def modulation(which):
        columns = slice(which * width, (which + 1) * width)
        return dot_nn(onehot, parts[:, columns]) + table_ref[which : which + 1, :]

    inputs_f = input_ref[...].astype(F32)
    centered = inputs_f - jnp.mean(inputs_f, axis=1, keepdims=True)
    inverse = lax.rsqrt(jnp.mean(centered * centered, axis=1, keepdims=True) + EPSILON)
    normed = centered * inverse
    normed_ref[...] = normed
    scale = 1.0 + modulation(1)
    scale_ref[...] = scale
    modded = (normed * scale + modulation(0)).astype(BF16)
    modded_ref[...] = modded
    gated = (modulation(2) * cotangent_ref[...].astype(F32)).astype(BF16)
    gated_ref[...] = gated
    down.wait()
    low_in_ref[...] = dot_nn(modded, down_ref[...]).astype(BF16)
    up.wait()
    low_grad_ref[...] = dot_nn(gated, up_ref[...]).astype(BF16)


def forward_kernel(
    place_ref, frames_ref, sizes_ref, layout_ref, low_grad_ref, saved_in_ref, gated_in_ref,
    cotangent_in_ref, adapters_ref, attention_ref, low_out_ref, gate_ref, grad_down_ref, grad_up_ref,
    bias_ref, level_ref, down_ref, up_ref, saved_ref, gated_ref, cotangent_ref, sems,
):
    rows, inner = attention_ref.shape
    width = up_ref.shape[0]
    count = adapters_ref.shape[1]
    down = pltpu.make_async_copy(
        adapters_ref.at[0, count - width - inner : count - width, :], down_ref, sems.at[0]
    )
    up = pltpu.make_async_copy(adapters_ref.at[0, count - width :, :], up_ref, sems.at[1])
    factor = HEAD ** (-0.5)
    group = 3
    held = []
    for n, start in enumerate(range(0, inner, group * HEAD)):
        stop = min(start + group * HEAD, inner)
        for part in range(3):
            columns = slice(part * inner + start, part * inner + stop)
            held.append(
                pltpu.make_async_copy(
                    saved_in_ref.at[:, columns], saved_ref.at[:, columns], sems.at[4 + 3 * n + part]
                )
            )
    gated_copy = pltpu.make_async_copy(gated_in_ref, gated_ref, sems.at[2])
    cotangent_copy = pltpu.make_async_copy(cotangent_in_ref, cotangent_ref, sems.at[3])
    for copy in held + [down, gated_copy, cotangent_copy, up]:
        copy.start()
    bias_ref[...] = mask_bias(frames_ref, sizes_ref, layout_ref, rows)
    for start in range(0, inner // HEAD, group):
        heads = range(start, min(start + group, inner // HEAD))
        for copy in held[start // group * 3 : start // group * 3 + 3]:
            copy.wait()
        scores = []
        for head in heads:
            query = saved_ref[:, head * HEAD : (head + 1) * HEAD]
            key = saved_ref[:, inner + head * HEAD : inner + (head + 1) * HEAD]
            scores.append(contract_last(key, query) * factor + bias_ref[...])
        probs = []
        for head, score in zip(heads, scores):
            most = jnp.max(score, axis=0, keepdims=True)
            raised = jnp.exp(score - most)
            whole = jnp.sum(raised, axis=0, keepdims=True)
            level_ref[head : head + 1, :] = most + jnp.log(whole)
            probs.append((raised * (1.0 / whole)).astype(BF16))
        for head, prob in zip(heads, probs):
            value = saved_ref[:, 2 * inner + head * HEAD : 2 * inner + (head + 1) * HEAD]
            attention_ref[:, head * HEAD : (head + 1) * HEAD] = contract_first(prob, value).astype(BF16)
    down.wait()
    attention = attention_ref[...]
    low_out = dot_nn(attention, down_ref[...]).astype(BF16)
    low_out_ref[...] = low_out
    grad_down_ref[...] = contract_first(attention, low_grad_ref[...])
    gated_copy.wait()
    grad_up_ref[...] = contract_first(gated_ref[...], low_out)
    up.wait()
    cotangent_copy.wait()
    branch = contract_last(low_out, up_ref[...])
    gate_ref[...] = jnp.sum(branch * cotangent_ref[...].astype(F32), axis=0, keepdims=True)


def layer_of(place_ref, step):
    ring = place_ref[2]
    return lax.rem(place_ref[0] - step + ring, ring)


def shard_copies(place_ref, shards, whole_ref, sems):
    copies = []
    for pieces, flip in zip(shards, (0, 2, 1, 3)):
        owner = (place_ref[1] ^ flip) * (whole_ref.shape[0] // 4)
        offset = 0
        for piece in pieces:
            start = pl.multiple_of(owner + offset, 16)
            offset += piece.shape[0]
            target = whole_ref.at[pl.ds(start, piece.shape[0]), :]
            copies.append(pltpu.make_async_copy(piece, target, sems.at[len(copies)]))
    return copies


def nested(refs, sizes):
    refs = list(refs)
    return [[refs.pop(0) for _ in range(size)] for size in sizes]


def backward_kernel(
    step, sizes,
    place_ref, low_grad_ref, low_in_ref, bias_ref, level_ref, gate_in_ref, total_in_ref,
    gated_in_ref, cotangent_in_ref, saved_ref, attention_ref, adapters_ref, *refs,
):
    shards = nested(refs, sizes)
    refs = refs[sum(sizes) :]
    grad_ref, grad_up_ref, gate_ref, total_ref = refs[:4]
    whole_ref, held_ref, out_ref, down_ref, up_ref, gated_ref, cotangent_ref, sems = refs[4:]
    depth, width = whole_ref.shape
    inner = attention_ref.shape[1]
    first = pl.multiple_of(layer_of(place_ref, step) * depth, HEAD)
    layer = pl.ds(first, depth)
    weights = shard_copies(place_ref, shards, whole_ref, sems)
    used = len(weights)
    parts = [pl.ds(pl.multiple_of(part * inner + first, HEAD), depth) for part in range(3)]
    held = [
        pltpu.make_async_copy(saved_ref.at[:, parts[part]], held_ref.at[part], sems.at[used + part])
        for part in range(3)
    ]
    others = [
        pltpu.make_async_copy(gated_in_ref, gated_ref, sems.at[used + 8]),
        pltpu.make_async_copy(cotangent_in_ref, cotangent_ref, sems.at[used + 9]),
        pltpu.make_async_copy(attention_ref.at[:, layer], out_ref, sems.at[used + 3]),
        pltpu.make_async_copy(
            adapters_ref.at[0, pl.ds(pl.multiple_of(width + 3 * inner + first, HEAD), depth), :],
            down_ref,
            sems.at[used + 4],
        ),
    ] + [
        pltpu.make_async_copy(
            adapters_ref.at[0, pl.ds(pl.multiple_of(width + part * inner + first, HEAD), depth), :],
            up_ref.at[pl.ds(part * depth, depth), :],
            sems.at[used + 5 + part],
        )
        for part in range(3)
    ]
    for copy in held + weights + others:
        copy.start()
    factor = HEAD ** (-0.5)
    heads = range(depth // HEAD)
    spans = [slice(head * HEAD, (head + 1) * HEAD) for head in heads]
    for copy in held:
        copy.wait()
    probs = []
    for head in heads:
        scores = contract_last(held_ref[1, :, spans[head]], held_ref[0, :, spans[head]]) * factor
        level = level_ref[pl.ds(layer_of(place_ref, step) * len(heads) + head, 1), :]
        probs.append(jnp.exp(scores + (bias_ref[...] - level)))
    for copy in weights + others:
        copy.wait()
    grad_attention = (
        contract_last(gated_ref[...], whole_ref[...])
        + contract_last(low_grad_ref[...], down_ref[...])
    ).astype(BF16)
    grad_scores = []
    for head in heads:
        grad = grad_attention[:, spans[head]]
        grad_probs = contract_last(held_ref[2, :, spans[head]], grad)
        delta = jnp.sum(probs[head] * grad_probs, axis=0, keepdims=True)
        grad_scores.append((probs[head] * ((grad_probs - delta) * factor)).astype(BF16))
    for head in heads:
        grad = grad_attention[:, spans[head]]
        pieces = (
            contract_first(grad_scores[head], held_ref[1, :, spans[head]]),
            dot_nn(grad_scores[head], held_ref[0, :, spans[head]]),
            dot_nn(probs[head].astype(BF16), grad),
        )
        for part, piece in enumerate(pieces):
            columns = slice(part * depth + head * HEAD, part * depth + (head + 1) * HEAD)
            grad_ref[:, columns] = piece.astype(BF16)
    grads = grad_ref[...]
    grad_up_ref[...] = contract_first(grads, low_in_ref[...])
    total_ref[...] = total_in_ref[...] + dot_nn(grads, up_ref[...])
    branch = dot_nn(out_ref[...], whole_ref[...])
    gate_ref[...] = gate_in_ref[...] + jnp.sum(
        branch * cotangent_ref[...].astype(F32), axis=0, keepdims=True
    )


def adapter_kernel(
    ring, place_ref, modded_ref, total_ref, grad_down_ref, grad_up_ref, *refs,
):
    layer_refs, (low_ref, sent_ref, kept_ref, whole_ref) = refs[:ring], refs[ring:]
    width = modded_ref.shape[1]
    inner = grad_down_ref.shape[0]
    depth = inner // ring
    low = total_ref[...].astype(BF16)
    low_ref[...] = low
    whole_ref[:width, :] = contract_first(modded_ref[...], low)
    for step in range(ring):
        first = layer_of(place_ref, step) * depth
        for part in range(3):
            start = pl.multiple_of(width + part * inner + first, HEAD)
            whole_ref[pl.ds(start, depth), :] = layer_refs[step][part * depth : (part + 1) * depth, :]
    whole_ref[width + 3 * inner : width + 4 * inner, :] = grad_down_ref[...]
    whole_ref[width + 4 * inner :, :] = grad_up_ref[...]
    blocks, block = kept_ref.shape[0], kept_ref.shape[1]
    lane = place_ref[1] % 2
    for j in range(blocks):
        mine = pl.multiple_of((2 * j + lane) * block, 64)
        other = pl.multiple_of((2 * j + 1 - lane) * block, 64)
        kept_ref[j] = whole_ref[pl.ds(mine, block), :]
        sent_ref[j] = whole_ref[pl.ds(other, block), :].astype(BF16)


def input_kernel(
    step, ring, sizes, place_ref, low_ref, table_in_ref, *refs,
):
    grad_refs, refs = refs[:ring], refs[ring:]
    normed_ref, scale_ref, adapters_ref = refs[:3]
    shards = nested(refs[3:], sizes)
    u_ref, table_ref, whole_ref, near_ref, down_ref, held_ref, sems = refs[3 + sum(sizes) :]
    depth = whole_ref.shape[0]
    inner = whole_ref.shape[1] // 3
    first = pl.multiple_of(layer_of(place_ref, step) * depth, HEAD)
    layer = pl.ds(first, depth)
    count = sum(sizes)
    parts = []
    for part in range(3):
        columns = slice(part * inner, (part + 1) * inner)
        near = [[piece.at[:, columns] for piece in shard] for shard in shards]
        copies = shard_copies(
            place_ref, near, whole_ref.at[:, columns], sems.at[pl.ds(part * (count + ring), count)]
        )
        for n in range(ring):
            start = pl.multiple_of(part * inner + layer_of(place_ref, n) * depth, HEAD)
            copies.append(
                pltpu.make_async_copy(
                    grad_refs[n].at[:, part * depth : (part + 1) * depth],
                    held_ref.at[:, pl.ds(start, depth)],
                    sems.at[part * (count + ring) + count + n],
                )
            )
        parts.append(copies)
    used = 3 * (count + ring)
    others = [
        pltpu.make_async_copy(adapters_ref.at[0, layer, :], down_ref, sems.at[used]),
        pltpu.make_async_copy(normed_ref.at[:, layer], near_ref.at[0], sems.at[used + 1]),
        pltpu.make_async_copy(scale_ref.at[:, layer], near_ref.at[1], sems.at[used + 2]),
    ]
    for copy in sum(parts, []) + others:
        copy.start()
    total = jnp.zeros(u_ref.shape, F32)
    for part in range(3):
        for copy in parts[part]:
            copy.wait()
        columns = slice(part * inner, (part + 1) * inner)
        total = total + contract_last(held_ref[:, columns], whole_ref[:, columns])
    for copy in others:
        copy.wait()
    total = total + contract_last(low_ref[...], down_ref[...])
    u_ref[...] = (total * near_ref[1]).astype(BF16)
    table_ref[...] = table_in_ref[...]
    table_ref[0:1, layer] = jnp.sum(total, axis=0, keepdims=True)
    table_ref[1:2, layer] = jnp.sum(total * near_ref[0], axis=0, keepdims=True)


def finish_kernel(ring, place_ref, input_ref, cotangent_ref, *refs):
    u_refs, (out_ref, u_ref) = refs[:ring], refs[ring:]
    depth = u_refs[0].shape[1]
    for step in range(ring):
        layer = pl.ds(pl.multiple_of(layer_of(place_ref, step) * depth, HEAD), depth)
        u_ref[:, layer] = u_refs[step][...].astype(F32)
    inputs_f = input_ref[...].astype(F32)
    centered = inputs_f - jnp.mean(inputs_f, axis=1, keepdims=True)
    inverse = lax.rsqrt(jnp.mean(centered * centered, axis=1, keepdims=True) + EPSILON)
    normed = centered * inverse
    u = u_ref[...]
    out_ref[...] = (
        cotangent_ref[...].astype(F32)
        + inverse
        * (
            u
            - jnp.mean(u, axis=1, keepdims=True)
            - normed * jnp.mean(u * normed, axis=1, keepdims=True)
        )
    ).astype(BF16)


def call(kernel, outs, specs, operands, time, scratch=(), name=None):
    space = {"s": pltpu.SMEM, "v": pltpu.VMEM, "a": pl.ANY}
    return pl.pallas_call(
        kernel,
        out_shape=outs,
        in_specs=[pl.BlockSpec(memory_space=space[s]) for s in specs],
        out_specs=[pl.BlockSpec(memory_space=pltpu.VMEM)] * len(outs),
        scratch_shapes=list(scratch),
        compiler_params=pltpu.CompilerParams(vmem_limit_bytes=VMEM_LIMIT),
        cost_estimate=pl.CostEstimate(flops=0, bytes_accessed=int(time * PACE), transcendentals=0),
        name=name,
    )(*operands)


def shape(*dims, dtype=BF16):
    return jax.ShapeDtypeStruct(dims, dtype)


def gate(value, *events):
    return lax.optimization_barrier((value, *events))[0]


def exchanged_sum(part, event):
    count = lax.axis_size("dp")
    total = part
    for flip in (1, 2, 3):
        total = total + swapped(part, flip)
    part = total
    for distance in range(4, count, 4):
        route = [(i, (i + distance) % count) for i in range(count)]
        total = total + gate(lax.ppermute(part, "dp", route), event)
    return total


def on_device(
    block_input,
    saved_qkv,
    cotangent,
    mod_table,
    clip_condition,
    clip_frames,
    frame_tokens,
    tile_layout,
    frozen_qkv,
    frozen_out,
    adapters,
):
    count = lax.axis_size("dp")
    depth = 4 * frozen_out.shape[1]
    if count != 16 or depth % HEAD or depth != 4 * frozen_qkv.shape[1]:
        return on_device_general(
            block_input, saved_qkv, cotangent, mod_table, clip_condition, clip_frames,
            frame_tokens, tile_layout, frozen_qkv, frozen_out, adapters,
        )
    ring = count // 4
    me = lax.axis_index("dp")
    place = jnp.stack([me // 4, me % 4, jnp.int32(ring)]).astype(jnp.int32)
    tokens_here, saved, cot = block_input[0], saved_qkv[0], cotangent[0]
    rows, width = tokens_here.shape
    inner = saved.shape[1] // 3
    rank = adapters.shape[2]
    heads = inner // HEAD
    stages = lax.axis_size("pipe")
    before = [((i + 1) % stages, i) for i in range(stages)]
    clips = [clip_frames, frame_tokens]
    beside = lambda block: swapped(block, 1)
    across = lambda block: swapped(block, 2)

    out_r, qkv_r = [frozen_out[0]], [frozen_qkv[0]]
    out_r.append(ring_shifted(out_r[0]))
    out_x = [across(out_r[0])]
    out_rc, out_xc, qkv_x, qkv_rc, qkv_xc = [beside(out_r[0])], [], [], [], []
    modded, gated, normed, scale, low_in, low_grad_out = call(
        pre_kernel,
        [shape(rows, width), shape(rows, width), shape(rows, width, dtype=F32),
         shape(rows, width, dtype=F32), shape(rows, rank), shape(rows, rank)],
        "sssvvvva",
        [place, *clips, tokens_here, cot, mod_table[0], clip_condition[0], adapters],
        4,
        scratch=[pltpu.VMEM((width, rank), BF16), pltpu.VMEM((width, rank), BF16), pltpu.SemaphoreType.DMA((2,))],
        name="modulate",
    )
    event = low_in
    out_r.append(ring_shifted(gate(out_r[1], event)))
    out_x.append(across(gate(out_r[1], event)))
    out_xc.append(beside(gate(out_x[0], event)))
    attention, low_out, gate_sum, grad_down_out, grad_up_out, bias, level = call(
        forward_kernel,
        [shape(rows, inner), shape(rows, rank), shape(1, width, dtype=F32),
         shape(inner, rank, dtype=F32), shape(width, rank, dtype=F32),
         shape(rows, rows, dtype=F32), shape(heads, rows, dtype=F32)],
        "ssssvaaaa",
        [gate(place, out_r[1], out_x[0]), *clips, tile_layout, low_grad_out, saved, gated, cot, adapters],
        6,
        scratch=[
            pltpu.VMEM((inner, rank), BF16), pltpu.VMEM((width, rank), BF16),
            pltpu.VMEM(saved.shape, BF16), pltpu.VMEM((rows, width), BF16),
            pltpu.VMEM((rows, width), BF16), pltpu.SemaphoreType.DMA((4 + 3 * heads,)),
        ],
        name="attend",
    )

    event = low_out

    def backward(step, gate_sum, total, *waited):
        shards = ([out_r[step]], [out_x[step]], [out_rc[step]], [out_xc[step]])
        return call(
            lambda *refs: backward_kernel(step, [1, 1, 1, 1], *refs),
            [shape(rows, 3 * depth), shape(3 * depth, rank, dtype=F32),
             shape(1, width, dtype=F32), shape(rows, rank, dtype=F32)],
            "svvvvvvaaaaaaaaa",
            [gate(place, *waited), low_grad_out, low_in, bias, level, gate_sum, total, gated, cot, saved,
             attention, adapters, *sum(shards, [])],
            5,
            scratch=[
                pltpu.VMEM((depth, width), BF16), pltpu.VMEM((3, rows, depth), BF16),
                pltpu.VMEM((rows, depth), BF16), pltpu.VMEM((depth, rank), BF16),
                pltpu.VMEM((3 * depth, rank), BF16), pltpu.VMEM((rows, width), BF16),
                pltpu.VMEM((rows, width), BF16), pltpu.SemaphoreType.DMA((14,)),
            ],
            name=f"backward{step}",
        )

    total = jnp.zeros((rows, rank), F32)
    out_r.append(ring_shifted(gate(out_r[2], event)))
    out_x.append(across(gate(out_r[2], event)))
    out_rc.append(beside(gate(out_r[1], event)))
    out_xc.append(beside(gate(out_x[1], event)))
    grad0, grad_up0, gate_sum, total = backward(0, gate_sum, total, out_r[2], out_x[1], out_xc[0])
    event = total
    out_x.append(across(gate(out_r[3], event)))
    qkv_r.append(ring_shifted(gate(qkv_r[0], event, out_r[3])))
    qkv_rc.append(beside(gate(qkv_r[0], event)))
    out_rc.append(beside(gate(out_r[2], event)))
    out_xc.append(beside(gate(out_x[2], event)))
    grad1, grad_up1, gate_sum, total = backward(1, gate_sum, total, out_r[3], out_x[2])
    event = total
    qkv_x.append(across(gate(qkv_r[0], event, out_x[3])))
    next_input = lax.ppermute(gate(tokens_here, event), "pipe", before)
    next_cot = lax.ppermute(gate(cot, event), "pipe", before)
    out_rc.append(beside(gate(out_r[3], event)))
    out_xc.append(beside(gate(out_x[3], event)))
    grad2, grad_up2, gate_sum, total = backward(2, gate_sum, total, out_x[3])
    grad3, grad_up3, gate_sum, total = backward(3, gate_sum, total)
    event = total
    grads = [grad0, grad1, grad2, grad3]
    grad_ups = [grad_up0, grad_up1, grad_up2, grad_up3]

    block = adapters.shape[1] // count
    low_grad_in, sent, kept = call(
        lambda *refs: adapter_kernel(ring, *refs),
        [shape(rows, rank), shape(count // 2, block, rank), shape(count // 2, block, rank, dtype=F32)],
        "svvvv" + "v" * ring,
        [place, modded, total, grad_down_out, grad_up_out, *grad_ups],
        4,
        scratch=[pltpu.VMEM(adapters.shape[1:], F32)],
        name="adapt",
    )

    def project(step, *waited):
        shards = layers[step]
        sizes = [len(shard) for shard in shards]
        return call(
            lambda *refs: input_kernel(step, ring, sizes, *refs),
            [shape(rows, depth), shape(3, width, dtype=F32)],
            "svv" + "a" * ring + "aaa" + "a" * sum(sizes),
            [gate(place, *waited), low_grad_in, table, *grads, normed, scale, adapters, *sum(shards, [])],
            5,
            scratch=[
                pltpu.VMEM((depth, 3 * inner), BF16), pltpu.VMEM((2, rows, depth), F32),
                pltpu.VMEM((depth, rank), BF16), pltpu.VMEM((rows, 3 * inner), BF16),
                pltpu.SemaphoreType.DMA((3 * (sum(sizes) + ring) + 3,)),
            ],
            name=f"project{step}",
        )

    def halved(kept, bit):
        mine = (me // bit) % 2
        pairs = kept.reshape(-1, 2, block, rank)
        sent = lax.dynamic_index_in_dim(pairs, 1 - mine, 1, keepdims=False).astype(BF16)
        return lax.dynamic_index_in_dim(pairs, mine, 1, keepdims=False), sent

    sends = lambda u: lax.ppermute(u, "pipe", before)
    event = low_grad_in
    qkv_r.append(ring_shifted(gate(qkv_r[1], event)))
    qkv_x.append(across(gate(qkv_r[1], event)))
    qkv_rc.append(beside(gate(qkv_r[1], event)))
    qkv_xc.append(beside(gate(qkv_x[0], event)))
    arrived = beside(sent)
    layers = [[[qkv_r[0]], [qkv_x[0]], [qkv_rc[0]], [qkv_xc[0]]]]
    table = jnp.concatenate([jnp.zeros((2, width), F32), gate_sum], axis=0)
    u0, table = project(0, qkv_xc[0], next_input)
    qkv_r.append(ring_shifted(gate(qkv_r[2], u0)))
    qkv_x.append(across(gate(qkv_r[2], u0)))
    qkv_rc.append(beside(gate(qkv_r[2], u0)))
    qkv_xc.append(beside(gate(qkv_x[1], u0)))
    kept, sent = halved(kept + gate(arrived, u0).astype(F32), 2)
    received = [sends(u0)]
    layers.append([[qkv_r[1]], [qkv_x[1]], [qkv_rc[1]], [qkv_xc[1]]])
    u1, table = project(1, qkv_xc[1], sent, received[0], next_cot)
    rest = [ring_shifted(gate(qkv_x[2], u1))]
    qkv_rc.append(beside(gate(qkv_r[3], u1)))
    qkv_xc.append(beside(gate(qkv_x[2], u1)))
    arrived = across(gate(sent, u1))
    received.append(sends(u1))
    layers.append([[qkv_r[2]], [qkv_x[2]], [qkv_rc[2]], [qkv_xc[2]]])
    u2, table = project(2, qkv_xc[2], received[1])
    layers.append([[qkv_r[3]], rest, [qkv_rc[3]], [beside(gate(piece, u2)) for piece in rest]])
    received.append(sends(u2))
    u3, table = project(3)
    kept, sent = halved(kept + gate(arrived, u2).astype(F32), 4)
    arrived = swapped(sent, 4)
    kept, sent = halved(kept + gate(arrived, u3).astype(F32), 8)
    arrived = swapped(sent, 8)
    received.append(sends(u3))

    (passed_back,) = call(
        lambda *refs: finish_kernel(ring, *refs),
        [shape(rows, width)],
        "svv" + "v" * ring,
        [place, next_input, next_cot, *received],
        4,
        scratch=[pltpu.VMEM((rows, width), F32)],
        name="finish",
    )
    table_sum = exchanged_sum(table, passed_back)
    adapter_sum = (kept + gate(arrived, passed_back).astype(F32))[0]
    return (passed_back[None], (table_sum / count)[None], (adapter_sum / count)[None])


def solution(mesh):
    placed = (
        P("pipe", "dp", None),
        P("pipe", "dp", None),
        P("pipe", "dp", None),
        P("pipe", None, None),
        P("pipe", "dp", None),
        P("pipe", "dp"),
        P("pipe", "dp"),
        P("pipe", "dp", None),
        P("pipe", "dp", None),
        P("pipe", "dp", None),
        P("pipe", None, None),
    )
    return jax.shard_map(
        on_device,
        mesh=mesh,
        in_specs=placed,
        out_specs=(P("pipe", "dp", None), P("pipe", None, None), P("pipe", "dp", None)),
        check_vma=False,
    )
```

```python
import jax
import jax.numpy as jnp
from jax import lax
from jax.experimental import pallas as pl
from jax.experimental.pallas import tpu as pltpu
from jax.sharding import PartitionSpec as P

HEAD = 128
TILE = 128


EPSILON = 1e-06
HIGH = lax.Precision.HIGHEST


def contract_last(left, right):
    return lax.dot_general(
        left, right, (((1,), (1,)), ((), ())), preferred_element_type=jnp.float32
    )


def contract_first(left, right):
    return lax.dot_general(
        left, right, (((0,), (0,)), ((), ())), preferred_element_type=jnp.float32
    )


def swapped(block, bit):
    devices = range(lax.axis_size("dp"))
    return lax.ppermute(block, "dp", [(i, i ^ bit) for i in devices])


def ring_shifted(block):
    count = lax.axis_size("dp")
    return lax.ppermute(block, "dp", [(i, (i + 4) % count) for i in range(count)])


def lane_gather(block):
    me = lax.axis_index("dp")
    count = lax.axis_size("dp")
    rows, columns = block.shape
    whole = jnp.zeros((count // 2 * rows, columns), block.dtype)
    here = block
    for step in range(count // 4):
        if step:
            here = ring_shifted(here)
        across = swapped(here, 2)
        chip = (me - 4 * step + count) % count // 2
        whole = lax.dynamic_update_slice(whole, here, (chip * rows, 0))
        whole = lax.dynamic_update_slice(whole, across, ((chip ^ 1) * rows, 0))
    return whole


def interleaved(mine, other, lane, rows):
    first = jnp.where(lane == 0, mine, other)
    second = jnp.where(lane == 0, other, mine)
    columns = mine.shape[1]
    both = jnp.stack([first.reshape(-1, rows, columns), second.reshape(-1, rows, columns)], axis=1)
    return both.reshape(-1, columns)


def scatter_sum(part):
    me = lax.axis_index("dp")
    count = lax.axis_size("dp")
    rows, columns = part.shape
    kept = part.reshape(count, rows // count, columns)
    bit = 1
    while bit < count:
        mine = (me // bit) % 2
        pairs = kept.reshape(-1, 2, rows // count, columns)
        sent = lax.dynamic_index_in_dim(pairs, 1 - mine, 1, keepdims=False).astype(jnp.bfloat16)
        kept = lax.dynamic_index_in_dim(pairs, mine, 1, keepdims=False)
        kept = kept + swapped(sent, bit).astype(jnp.float32)
        bit *= 2
    return kept[0]


def whole_sum(part):
    bit = 1
    while bit < lax.axis_size("dp"):
        part = part + swapped(part, bit)
        bit *= 2
    return part


def on_device_general(
    block_input,
    saved_qkv,
    cotangent,
    mod_table,
    clip_condition,
    clip_frames,
    frame_tokens,
    tile_layout,
    frozen_qkv,
    frozen_out,
    adapters,
):
    lane = lax.axis_index("dp") % 2
    tokens_here = block_input[0]
    rows, width = tokens_here.shape
    saved = saved_qkv[0]
    inner = saved.shape[1] // 3
    heads = inner // HEAD
    slots = clip_frames.shape[1]
    tiles = tile_layout.shape[1]
    adapter_rows = adapters[0]
    down_qkv = adapter_rows[:width]
    up_qkv = adapter_rows[width : width + 3 * inner]
    down_out = adapter_rows[width + 3 * inner : width + 4 * inner]
    up_out = adapter_rows[width + 4 * inner :]

    lane_out = lane_gather(frozen_out[0])
    out_whole = interleaved(lane_out, swapped(lane_out, 1), lane, frozen_out.shape[1])
    lane_qkv = lane_gather(frozen_qkv[0])

    clip_ends = jnp.cumsum(clip_frames[0] * frame_tokens[0])
    position = jnp.arange(rows, dtype=jnp.int32)
    clip_of = jnp.sum((position[:, None] >= clip_ends[None, :]).astype(jnp.int32), axis=1)
    onehot_clip = (clip_of[:, None] == jnp.arange(slots, dtype=jnp.int32)[None, :]).astype(
        jnp.float32
    )
    modulation = mod_table[0].reshape(1, 3 * width) + jnp.dot(
        onehot_clip, clip_condition[0], precision=HIGH
    )
    shift_rows = modulation[:, :width]
    scale_rows = modulation[:, width : 2 * width]
    gate_rows = modulation[:, 2 * width :]
    inputs_f = tokens_here.astype(jnp.float32)
    centered = inputs_f - jnp.mean(inputs_f, axis=1, keepdims=True)
    inverse = lax.rsqrt(jnp.mean(centered * centered, axis=1, keepdims=True) + EPSILON)
    normed = centered * inverse
    modded = (normed * (1.0 + scale_rows) + shift_rows).astype(jnp.bfloat16)
    tile_onehot = (
        (position // TILE)[:, None] == jnp.arange(tiles, dtype=jnp.int32)[None, :]
    ).astype(jnp.float32)
    live_rows = jnp.dot(tile_onehot, tile_layout[0].astype(jnp.float32), precision=HIGH)
    live_pairs = jnp.dot(live_rows, tile_onehot.T, precision=HIGH) > 0.5
    allowed = live_pairs & (clip_of[:, None] == clip_of[None, :])
    queries = saved[:, :inner].reshape(rows, heads, HEAD)
    key_rows = saved[:, inner : 2 * inner].reshape(rows, heads, HEAD)
    value_rows = saved[:, 2 * inner :].reshape(rows, heads, HEAD)
    factor = HEAD ** (-0.5)
    scores = (
        jnp.einsum("qhd,khd->hqk", queries, key_rows, preferred_element_type=jnp.float32) * factor
    )
    scores = jnp.where(allowed[None], scores, -jnp.inf)
    probs = jax.nn.softmax(scores, axis=2)
    probs_b = probs.astype(jnp.bfloat16)
    attention = (
        jnp.einsum("hqk,khd->qhd", probs_b, value_rows, preferred_element_type=jnp.float32)
        .reshape(rows, inner)
        .astype(jnp.bfloat16)
    )
    low_out = jnp.dot(attention, down_out, preferred_element_type=jnp.float32).astype(jnp.bfloat16)
    cotangent_f = cotangent[0].astype(jnp.float32)
    gated = (gate_rows * cotangent_f).astype(jnp.bfloat16)
    low_grad_out = jnp.dot(gated, up_out, preferred_element_type=jnp.float32).astype(jnp.bfloat16)
    low_in = jnp.dot(modded, down_qkv, preferred_element_type=jnp.float32).astype(jnp.bfloat16)
    branch = jnp.dot(attention, out_whole, preferred_element_type=jnp.float32) + contract_last(
        low_out, up_out
    )
    grad_attention = (
        contract_last(gated, out_whole) + contract_last(low_grad_out, down_out)
    ).astype(jnp.bfloat16)
    grad_heads = grad_attention.reshape(rows, heads, HEAD)
    grad_probs = jnp.einsum(
        "qhd,khd->hqk", grad_heads, value_rows, preferred_element_type=jnp.float32
    )
    delta = jnp.sum(probs * grad_probs, axis=2, keepdims=True)
    grad_scores = (probs * (grad_probs - delta) * factor).astype(jnp.bfloat16)
    grad_query = jnp.einsum(
        "hqk,khd->qhd", grad_scores, key_rows, preferred_element_type=jnp.float32
    ).reshape(rows, inner)
    grad_key = jnp.einsum(
        "hqk,qhd->khd", grad_scores, queries, preferred_element_type=jnp.float32
    ).reshape(rows, inner)
    grad_value = jnp.einsum(
        "hqk,qhd->khd", probs_b, grad_heads, preferred_element_type=jnp.float32
    ).reshape(rows, inner)
    grad_qkv = jnp.concatenate([grad_query, grad_key, grad_value], axis=1).astype(jnp.bfloat16)
    grad_beside = swapped(grad_qkv, 1)
    low_grad_in = jnp.dot(grad_qkv, up_qkv, preferred_element_type=jnp.float32).astype(jnp.bfloat16)
    adapter_part = jnp.concatenate(
        [
            contract_first(modded, low_grad_in),
            contract_first(grad_qkv, low_in),
            contract_first(attention, low_grad_out),
            contract_first(gated, low_out),
        ],
        axis=0,
    )
    replicas = lax.axis_size("dp")
    adapter_sum = scatter_sum(adapter_part)

    part_rows = frozen_qkv.shape[1]
    frozen_beside = swapped(contract_last(grad_beside, lane_qkv), 1)
    frozen_mine = contract_last(grad_qkv, lane_qkv)
    first = jnp.where(lane == 0, frozen_mine, frozen_beside).reshape(rows, -1, part_rows)
    second = jnp.where(lane == 0, frozen_beside, frozen_mine).reshape(rows, -1, part_rows)
    frozen_part = jnp.stack([first, second], axis=2).reshape(rows, width)
    grad_modded = frozen_part + contract_last(low_grad_in, down_qkv)
    grad_normed = grad_modded * (1.0 + scale_rows)
    grad_input = cotangent_f + inverse * (
        grad_normed
        - jnp.mean(grad_normed, axis=1, keepdims=True)
        - normed * jnp.mean(grad_normed * normed, axis=1, keepdims=True)
    )
    grad_input = grad_input.astype(jnp.bfloat16)
    table_part = jnp.stack(
        [
            jnp.sum(grad_modded, axis=0),
            jnp.sum(grad_modded * normed, axis=0),
            jnp.sum(cotangent_f * branch, axis=0),
        ]
    )
    stages = lax.axis_size("pipe")
    passed_back = lax.ppermute(
        grad_input, "pipe", [((i + 1) % stages, i) for i in range(stages)]
    )
    table_sum = whole_sum(table_part)
    return (passed_back[None], (table_sum / replicas)[None], (adapter_sum / replicas)[None])


VMEM_LIMIT = 58 * 1024 * 1024
PACE = 1.0e6
F32 = jnp.float32
BF16 = jnp.bfloat16


def dot_nn(left, right):
    return lax.dot_general(
        left, right, (((1,), (0,)), ((), ())), preferred_element_type=jnp.float32
    )


def clip_numbers(frames_ref, sizes_ref, position):
    clip = jnp.zeros_like(position)
    end = jnp.int32(0)
    for slot in range(frames_ref.shape[1]):
        end = end + frames_ref[0, slot] * sizes_ref[0, slot]
        clip = clip + (position >= end).astype(jnp.int32)
    return clip


def mask_bias(frames_ref, sizes_ref, layout_ref, rows):
    down = lax.broadcasted_iota(jnp.int32, (rows, 1), 0)
    across = lax.broadcasted_iota(jnp.int32, (1, rows), 1)
    same = clip_numbers(frames_ref, sizes_ref, down) == clip_numbers(frames_ref, sizes_ref, across)
    live = jnp.zeros((rows, rows), jnp.int32)
    for i in range(rows // TILE):
        for j in range(rows // TILE):
            inside = (across // TILE == i) & (down // TILE == j)
            live = jnp.where(inside, layout_ref[0, i, j], live)
    return jnp.where(same & (live > 0), 0.0, -jnp.inf).astype(jnp.float32)


def pre_kernel(
    place_ref, frames_ref, sizes_ref, input_ref, cotangent_ref, table_ref, condition_ref, adapters_ref,
    modded_ref, gated_ref, normed_ref, scale_ref, low_in_ref, low_grad_ref,
    down_ref, up_ref, sems,
):
    rows, width = input_ref.shape
    slots = condition_ref.shape[0]
    down = pltpu.make_async_copy(adapters_ref.at[0, :width, :], down_ref, sems.at[0])
    up = pltpu.make_async_copy(adapters_ref.at[0, adapters_ref.shape[1] - width :, :], up_ref, sems.at[1])
    down.start()
    up.start()
    position = lax.broadcasted_iota(jnp.int32, (rows, 1), 0)
    clip = clip_numbers(frames_ref, sizes_ref, position)
    whole = condition_ref[...]
    high = whole.astype(BF16)
    rest = whole - high.astype(F32)
    middle = rest.astype(BF16)
    low = (rest - middle.astype(F32)).astype(BF16)
    parts = jnp.concatenate([high.astype(F32), middle.astype(F32), low.astype(F32)], axis=0)
    lanes = lax.broadcasted_iota(jnp.int32, (rows, 3 * slots), 1) % slots
    onehot = (clip == lanes).astype(F32).astype(BF16)
    parts = parts.astype(BF16)

    def modulation(which):
        columns = slice(which * width, (which + 1) * width)
        return dot_nn(onehot, parts[:, columns]) + table_ref[which : which + 1, :]

    inputs_f = input_ref[...].astype(F32)
    centered = inputs_f - jnp.mean(inputs_f, axis=1, keepdims=True)
    inverse = lax.rsqrt(jnp.mean(centered * centered, axis=1, keepdims=True) + EPSILON)
    normed = centered * inverse
    normed_ref[...] = normed
    scale = 1.0 + modulation(1)
    scale_ref[...] = scale
    modded = (normed * scale + modulation(0)).astype(BF16)
    modded_ref[...] = modded
    gated = (modulation(2) * cotangent_ref[...].astype(F32)).astype(BF16)
    gated_ref[...] = gated
    down.wait()
    low_in_ref[...] = dot_nn(modded, down_ref[...]).astype(BF16)
    up.wait()
    low_grad_ref[...] = dot_nn(gated, up_ref[...]).astype(BF16)


def forward_kernel(
    place_ref, frames_ref, sizes_ref, layout_ref, low_grad_ref, saved_in_ref, gated_in_ref,
    cotangent_in_ref, adapters_ref, attention_ref, low_out_ref, gate_ref, grad_down_ref, grad_up_ref,
    bias_ref, level_ref, down_ref, up_ref, saved_ref, gated_ref, cotangent_ref, sems,
):
    rows, inner = attention_ref.shape
    width = up_ref.shape[0]
    count = adapters_ref.shape[1]
    down = pltpu.make_async_copy(
        adapters_ref.at[0, count - width - inner : count - width, :], down_ref, sems.at[0]
    )
    up = pltpu.make_async_copy(adapters_ref.at[0, count - width :, :], up_ref, sems.at[1])
    factor = HEAD ** (-0.5)
    group = 3
    held = []
    for n, start in enumerate(range(0, inner, group * HEAD)):
        stop = min(start + group * HEAD, inner)
        for part in range(3):
            columns = slice(part * inner + start, part * inner + stop)
            held.append(
                pltpu.make_async_copy(
                    saved_in_ref.at[:, columns], saved_ref.at[:, columns], sems.at[4 + 3 * n + part]
                )
            )
    gated_copy = pltpu.make_async_copy(gated_in_ref, gated_ref, sems.at[2])
    cotangent_copy = pltpu.make_async_copy(cotangent_in_ref, cotangent_ref, sems.at[3])
    for copy in held + [down, gated_copy, cotangent_copy, up]:
        copy.start()
    bias_ref[...] = mask_bias(frames_ref, sizes_ref, layout_ref, rows)
    for start in range(0, inner // HEAD, group):
        heads = range(start, min(start + group, inner // HEAD))
        for copy in held[start // group * 3 : start // group * 3 + 3]:
            copy.wait()
        scores = []
        for head in heads:
            query = saved_ref[:, head * HEAD : (head + 1) * HEAD]
            key = saved_ref[:, inner + head * HEAD : inner + (head + 1) * HEAD]
            scores.append(contract_last(key, query) * factor + bias_ref[...])
        probs = []
        for head, score in zip(heads, scores):
            most = jnp.max(score, axis=0, keepdims=True)
            raised = jnp.exp(score - most)
            whole = jnp.sum(raised, axis=0, keepdims=True)
            level_ref[head : head + 1, :] = most + jnp.log(whole)
            probs.append((raised * (1.0 / whole)).astype(BF16))
        for head, prob in zip(heads, probs):
            value = saved_ref[:, 2 * inner + head * HEAD : 2 * inner + (head + 1) * HEAD]
            attention_ref[:, head * HEAD : (head + 1) * HEAD] = contract_first(prob, value).astype(BF16)
    down.wait()
    attention = attention_ref[...]
    low_out = dot_nn(attention, down_ref[...]).astype(BF16)
    low_out_ref[...] = low_out
    grad_down_ref[...] = contract_first(attention, low_grad_ref[...])
    gated_copy.wait()
    grad_up_ref[...] = contract_first(gated_ref[...], low_out)
    up.wait()
    cotangent_copy.wait()
    branch = contract_last(low_out, up_ref[...])
    gate_ref[...] = jnp.sum(branch * cotangent_ref[...].astype(F32), axis=0, keepdims=True)


def layer_of(place_ref, step):
    ring = place_ref[2]
    return lax.rem(place_ref[0] - step + ring, ring)


def shard_copies(place_ref, shards, whole_ref, sems):
    copies = []
    for pieces, flip in zip(shards, (0, 2, 1, 3)):
        owner = (place_ref[1] ^ flip) * (whole_ref.shape[0] // 4)
        offset = 0
        for piece in pieces:
            start = pl.multiple_of(owner + offset, 16)
            offset += piece.shape[0]
            target = whole_ref.at[pl.ds(start, piece.shape[0]), :]
            copies.append(pltpu.make_async_copy(piece, target, sems.at[len(copies)]))
    return copies


def nested(refs, sizes):
    refs = list(refs)
    return [[refs.pop(0) for _ in range(size)] for size in sizes]


def backward_kernel(
    step, sizes,
    place_ref, low_grad_ref, low_in_ref, bias_ref, level_ref, gate_in_ref, total_in_ref,
    gated_in_ref, cotangent_in_ref, saved_ref, attention_ref, adapters_ref, *refs,
):
    shards = nested(refs, sizes)
    refs = refs[sum(sizes) :]
    grad_ref, grad_up_ref, gate_ref, total_ref = refs[:4]
    whole_ref, held_ref, out_ref, down_ref, up_ref, gated_ref, cotangent_ref, sems = refs[4:]
    depth, width = whole_ref.shape
    inner = attention_ref.shape[1]
    first = pl.multiple_of(layer_of(place_ref, step) * depth, HEAD)
    layer = pl.ds(first, depth)
    weights = shard_copies(place_ref, shards, whole_ref, sems)
    used = len(weights)
    parts = [pl.ds(pl.multiple_of(part * inner + first, HEAD), depth) for part in range(3)]
    held = [
        pltpu.make_async_copy(saved_ref.at[:, parts[part]], held_ref.at[part], sems.at[used + part])
        for part in range(3)
    ]
    others = [
        pltpu.make_async_copy(gated_in_ref, gated_ref, sems.at[used + 8]),
        pltpu.make_async_copy(cotangent_in_ref, cotangent_ref, sems.at[used + 9]),
        pltpu.make_async_copy(attention_ref.at[:, layer], out_ref, sems.at[used + 3]),
        pltpu.make_async_copy(
            adapters_ref.at[0, pl.ds(pl.multiple_of(width + 3 * inner + first, HEAD), depth), :],
            down_ref,
            sems.at[used + 4],
        ),
    ] + [
        pltpu.make_async_copy(
            adapters_ref.at[0, pl.ds(pl.multiple_of(width + part * inner + first, HEAD), depth), :],
            up_ref.at[pl.ds(part * depth, depth), :],
            sems.at[used + 5 + part],
        )
        for part in range(3)
    ]
    for copy in held + weights + others:
        copy.start()
    factor = HEAD ** (-0.5)
    heads = range(depth // HEAD)
    spans = [slice(head * HEAD, (head + 1) * HEAD) for head in heads]
    for copy in held:
        copy.wait()
    probs = []
    for head in heads:
        scores = contract_last(held_ref[1, :, spans[head]], held_ref[0, :, spans[head]]) * factor
        level = level_ref[pl.ds(layer_of(place_ref, step) * len(heads) + head, 1), :]
        probs.append(jnp.exp(scores + (bias_ref[...] - level)))
    for copy in weights + others:
        copy.wait()
    grad_attention = (
        contract_last(gated_ref[...], whole_ref[...])
        + contract_last(low_grad_ref[...], down_ref[...])
    ).astype(BF16)
    grad_scores = []
    for head in heads:
        grad = grad_attention[:, spans[head]]
        grad_probs = contract_last(held_ref[2, :, spans[head]], grad)
        delta = jnp.sum(probs[head] * grad_probs, axis=0, keepdims=True)
        grad_scores.append((probs[head] * ((grad_probs - delta) * factor)).astype(BF16))
    for head in heads:
        grad = grad_attention[:, spans[head]]
        pieces = (
            contract_first(grad_scores[head], held_ref[1, :, spans[head]]),
            dot_nn(grad_scores[head], held_ref[0, :, spans[head]]),
            dot_nn(probs[head].astype(BF16), grad),
        )
        for part, piece in enumerate(pieces):
            columns = slice(part * depth + head * HEAD, part * depth + (head + 1) * HEAD)
            grad_ref[:, columns] = piece.astype(BF16)
    grads = grad_ref[...]
    grad_up_ref[...] = contract_first(grads, low_in_ref[...])
    total_ref[...] = total_in_ref[...] + dot_nn(grads, up_ref[...])
    branch = dot_nn(out_ref[...], whole_ref[...])
    gate_ref[...] = gate_in_ref[...] + jnp.sum(
        branch * cotangent_ref[...].astype(F32), axis=0, keepdims=True
    )


def adapter_kernel(
    ring, place_ref, modded_ref, total_ref, grad_down_ref, grad_up_ref, *refs,
):
    layer_refs, (low_ref, sent_ref, kept_ref, whole_ref) = refs[:ring], refs[ring:]
    width = modded_ref.shape[1]
    inner = grad_down_ref.shape[0]
    depth = inner // ring
    low = total_ref[...].astype(BF16)
    low_ref[...] = low
    whole_ref[:width, :] = contract_first(modded_ref[...], low)
    for step in range(ring):
        first = layer_of(place_ref, step) * depth
        for part in range(3):
            start = pl.multiple_of(width + part * inner + first, HEAD)
            whole_ref[pl.ds(start, depth), :] = layer_refs[step][part * depth : (part + 1) * depth, :]
    whole_ref[width + 3 * inner : width + 4 * inner, :] = grad_down_ref[...]
    whole_ref[width + 4 * inner :, :] = grad_up_ref[...]
    blocks, block = kept_ref.shape[0], kept_ref.shape[1]
    lane = place_ref[1] % 2
    for j in range(blocks):
        mine = pl.multiple_of((2 * j + lane) * block, 64)
        other = pl.multiple_of((2 * j + 1 - lane) * block, 64)
        kept_ref[j] = whole_ref[pl.ds(mine, block), :]
        sent_ref[j] = whole_ref[pl.ds(other, block), :].astype(BF16)


def input_kernel(
    step, ring, sizes, place_ref, low_ref, table_in_ref, *refs,
):
    grad_refs, refs = refs[:ring], refs[ring:]
    normed_ref, scale_ref, adapters_ref = refs[:3]
    shards = nested(refs[3:], sizes)
    u_ref, table_ref, whole_ref, near_ref, down_ref, held_ref, sems = refs[3 + sum(sizes) :]
    depth = whole_ref.shape[0]
    inner = whole_ref.shape[1] // 3
    first = pl.multiple_of(layer_of(place_ref, step) * depth, HEAD)
    layer = pl.ds(first, depth)
    count = sum(sizes)
    parts = []
    for part in range(3):
        columns = slice(part * inner, (part + 1) * inner)
        near = [[piece.at[:, columns] for piece in shard] for shard in shards]
        copies = shard_copies(
            place_ref, near, whole_ref.at[:, columns], sems.at[pl.ds(part * (count + ring), count)]
        )
        for n in range(ring):
            start = pl.multiple_of(part * inner + layer_of(place_ref, n) * depth, HEAD)
            copies.append(
                pltpu.make_async_copy(
                    grad_refs[n].at[:, part * depth : (part + 1) * depth],
                    held_ref.at[:, pl.ds(start, depth)],
                    sems.at[part * (count + ring) + count + n],
                )
            )
        parts.append(copies)
    used = 3 * (count + ring)
    others = [
        pltpu.make_async_copy(adapters_ref.at[0, layer, :], down_ref, sems.at[used]),
        pltpu.make_async_copy(normed_ref.at[:, layer], near_ref.at[0], sems.at[used + 1]),
        pltpu.make_async_copy(scale_ref.at[:, layer], near_ref.at[1], sems.at[used + 2]),
    ]
    for copy in sum(parts, []) + others:
        copy.start()
    total = jnp.zeros(u_ref.shape, F32)
    for part in range(3):
        for copy in parts[part]:
            copy.wait()
        columns = slice(part * inner, (part + 1) * inner)
        total = total + contract_last(held_ref[:, columns], whole_ref[:, columns])
    for copy in others:
        copy.wait()
    total = total + contract_last(low_ref[...], down_ref[...])
    u_ref[...] = (total * near_ref[1]).astype(BF16)
    table_ref[...] = table_in_ref[...]
    table_ref[0:1, layer] = jnp.sum(total, axis=0, keepdims=True)
    table_ref[1:2, layer] = jnp.sum(total * near_ref[0], axis=0, keepdims=True)


def finish_kernel(ring, place_ref, input_ref, cotangent_ref, *refs):
    u_refs, (out_ref, u_ref) = refs[:ring], refs[ring:]
    depth = u_refs[0].shape[1]
    for step in range(ring):
        layer = pl.ds(pl.multiple_of(layer_of(place_ref, step) * depth, HEAD), depth)
        u_ref[:, layer] = u_refs[step][...].astype(F32)
    inputs_f = input_ref[...].astype(F32)
    centered = inputs_f - jnp.mean(inputs_f, axis=1, keepdims=True)
    inverse = lax.rsqrt(jnp.mean(centered * centered, axis=1, keepdims=True) + EPSILON)
    normed = centered * inverse
    u = u_ref[...]
    out_ref[...] = (
        cotangent_ref[...].astype(F32)
        + inverse
        * (
            u
            - jnp.mean(u, axis=1, keepdims=True)
            - normed * jnp.mean(u * normed, axis=1, keepdims=True)
        )
    ).astype(BF16)


def call(kernel, outs, specs, operands, time, scratch=(), name=None):
    space = {"s": pltpu.SMEM, "v": pltpu.VMEM, "a": pl.ANY}
    return pl.pallas_call(
        kernel,
        out_shape=outs,
        in_specs=[pl.BlockSpec(memory_space=space[s]) for s in specs],
        out_specs=[pl.BlockSpec(memory_space=pltpu.VMEM)] * len(outs),
        scratch_shapes=list(scratch),
        compiler_params=pltpu.CompilerParams(vmem_limit_bytes=VMEM_LIMIT),
        cost_estimate=pl.CostEstimate(flops=0, bytes_accessed=int(time * PACE), transcendentals=0),
        name=name,
    )(*operands)


def shape(*dims, dtype=BF16):
    return jax.ShapeDtypeStruct(dims, dtype)


def gate(value, *events):
    return lax.optimization_barrier((value, *events))[0]


def exchanged_sum(part, event):
    count = lax.axis_size("dp")
    total = part
    for flip in (1, 2, 3):
        total = total + swapped(part, flip)
    part = total
    for distance in range(4, count, 4):
        route = [(i, (i + distance) % count) for i in range(count)]
        total = total + gate(lax.ppermute(part, "dp", route), event)
    return total


def on_device(
    block_input,
    saved_qkv,
    cotangent,
    mod_table,
    clip_condition,
    clip_frames,
    frame_tokens,
    tile_layout,
    frozen_qkv,
    frozen_out,
    adapters,
):
    count = lax.axis_size("dp")
    depth = 4 * frozen_out.shape[1]
    if count != 16 or depth % HEAD or depth != 4 * frozen_qkv.shape[1]:
        return on_device_general(
            block_input, saved_qkv, cotangent, mod_table, clip_condition, clip_frames,
            frame_tokens, tile_layout, frozen_qkv, frozen_out, adapters,
        )
    ring = count // 4
    me = lax.axis_index("dp")
    place = jnp.stack([me // 4, me % 4, jnp.int32(ring)]).astype(jnp.int32)
    tokens_here, saved, cot = block_input[0], saved_qkv[0], cotangent[0]
    rows, width = tokens_here.shape
    inner = saved.shape[1] // 3
    rank = adapters.shape[2]
    heads = inner // HEAD
    stages = lax.axis_size("pipe")
    before = [((i + 1) % stages, i) for i in range(stages)]
    clips = [clip_frames, frame_tokens]
    beside = lambda block: swapped(block, 1)
    across = lambda block: swapped(block, 2)

    out_r, qkv_r = [frozen_out[0]], [frozen_qkv[0]]
    out_r.append(ring_shifted(out_r[0]))
    out_x = [across(out_r[0])]
    out_rc, out_xc, qkv_x, qkv_rc, qkv_xc = [beside(out_r[0])], [], [], [], []
    modded, gated, normed, scale, low_in, low_grad_out = call(
        pre_kernel,
        [shape(rows, width), shape(rows, width), shape(rows, width, dtype=F32),
         shape(rows, width, dtype=F32), shape(rows, rank), shape(rows, rank)],
        "sssvvvva",
        [place, *clips, tokens_here, cot, mod_table[0], clip_condition[0], adapters],
        4,
        scratch=[pltpu.VMEM((width, rank), BF16), pltpu.VMEM((width, rank), BF16), pltpu.SemaphoreType.DMA((2,))],
        name="modulate",
    )
    event = low_in
    out_r.append(ring_shifted(gate(out_r[1], event)))
    out_x.append(across(gate(out_r[1], event)))
    out_xc.append(beside(gate(out_x[0], event)))
    attention, low_out, gate_sum, grad_down_out, grad_up_out, bias, level = call(
        forward_kernel,
        [shape(rows, inner), shape(rows, rank), shape(1, width, dtype=F32),
         shape(inner, rank, dtype=F32), shape(width, rank, dtype=F32),
         shape(rows, rows, dtype=F32), shape(heads, rows, dtype=F32)],
        "ssssvaaaa",
        [gate(place, out_r[1], out_x[0]), *clips, tile_layout, low_grad_out, saved, gated, cot, adapters],
        6,
        scratch=[
            pltpu.VMEM((inner, rank), BF16), pltpu.VMEM((width, rank), BF16),
            pltpu.VMEM(saved.shape, BF16), pltpu.VMEM((rows, width), BF16),
            pltpu.VMEM((rows, width), BF16), pltpu.SemaphoreType.DMA((4 + 3 * heads,)),
        ],
        name="attend",
    )

    event = low_out

    def backward(step, gate_sum, total, *waited):
        shards = ([out_r[step]], [out_x[step]], [out_rc[step]], [out_xc[step]])
        return call(
            lambda *refs: backward_kernel(step, [1, 1, 1, 1], *refs),
            [shape(rows, 3 * depth), shape(3 * depth, rank, dtype=F32),
             shape(1, width, dtype=F32), shape(rows, rank, dtype=F32)],
            "svvvvvvaaaaaaaaa",
            [gate(place, *waited), low_grad_out, low_in, bias, level, gate_sum, total, gated, cot, saved,
             attention, adapters, *sum(shards, [])],
            5,
            scratch=[
                pltpu.VMEM((depth, width), BF16), pltpu.VMEM((3, rows, depth), BF16),
                pltpu.VMEM((rows, depth), BF16), pltpu.VMEM((depth, rank), BF16),
                pltpu.VMEM((3 * depth, rank), BF16), pltpu.VMEM((rows, width), BF16),
                pltpu.VMEM((rows, width), BF16), pltpu.SemaphoreType.DMA((14,)),
            ],
            name=f"backward{step}",
        )

    total = jnp.zeros((rows, rank), F32)
    out_r.append(ring_shifted(gate(out_r[2], event)))
    out_x.append(across(gate(out_r[2], event)))
    out_rc.append(beside(gate(out_r[1], event)))
    out_xc.append(beside(gate(out_x[1], event)))
    grad0, grad_up0, gate_sum, total = backward(0, gate_sum, total, out_r[2], out_x[1], out_xc[0])
    event = total
    out_x.append(across(gate(out_r[3], event)))
    qkv_r.append(ring_shifted(gate(qkv_r[0], event, out_r[3])))
    qkv_rc.append(beside(gate(qkv_r[0], event)))
    out_rc.append(beside(gate(out_r[2], event)))
    out_xc.append(beside(gate(out_x[2], event)))
    grad1, grad_up1, gate_sum, total = backward(1, gate_sum, total, out_r[3], out_x[2])
    event = total
    qkv_x.append(across(gate(qkv_r[0], event, out_x[3])))
    next_input = lax.ppermute(gate(tokens_here, event), "pipe", before)
    next_cot = lax.ppermute(gate(cot, event), "pipe", before)
    out_rc.append(beside(gate(out_r[3], event)))
    out_xc.append(beside(gate(out_x[3], event)))
    grad2, grad_up2, gate_sum, total = backward(2, gate_sum, total, out_x[3])
    grad3, grad_up3, gate_sum, total = backward(3, gate_sum, total)
    event = total
    grads = [grad0, grad1, grad2, grad3]
    grad_ups = [grad_up0, grad_up1, grad_up2, grad_up3]

    block = adapters.shape[1] // count
    low_grad_in, sent, kept = call(
        lambda *refs: adapter_kernel(ring, *refs),
        [shape(rows, rank), shape(count // 2, block, rank), shape(count // 2, block, rank, dtype=F32)],
        "svvvv" + "v" * ring,
        [place, modded, total, grad_down_out, grad_up_out, *grad_ups],
        4,
        scratch=[pltpu.VMEM(adapters.shape[1:], F32)],
        name="adapt",
    )

    def project(step, *waited):
        shards = layers[step]
        sizes = [len(shard) for shard in shards]
        return call(
            lambda *refs: input_kernel(step, ring, sizes, *refs),
            [shape(rows, depth), shape(3, width, dtype=F32)],
            "svv" + "a" * ring + "aaa" + "a" * sum(sizes),
            [gate(place, *waited), low_grad_in, table, *grads, normed, scale, adapters, *sum(shards, [])],
            5,
            scratch=[
                pltpu.VMEM((depth, 3 * inner), BF16), pltpu.VMEM((2, rows, depth), F32),
                pltpu.VMEM((depth, rank), BF16), pltpu.VMEM((rows, 3 * inner), BF16),
                pltpu.SemaphoreType.DMA((3 * (sum(sizes) + ring) + 3,)),
            ],
            name=f"project{step}",
        )

    def halved(kept, bit):
        mine = (me // bit) % 2
        pairs = kept.reshape(-1, 2, block, rank)
        sent = lax.dynamic_index_in_dim(pairs, 1 - mine, 1, keepdims=False).astype(BF16)
        return lax.dynamic_index_in_dim(pairs, mine, 1, keepdims=False), sent

    sends = lambda u: lax.ppermute(u, "pipe", before)
    event = low_grad_in
    qkv_r.append(ring_shifted(gate(qkv_r[1], event)))
    qkv_x.append(across(gate(qkv_r[1], event)))
    qkv_xc.append(beside(gate(qkv_x[0], event)))
    arrived = beside(sent)
    layers = [[[qkv_r[0]], [qkv_x[0]], [qkv_rc[0]], [qkv_xc[0]]]]
    table = jnp.concatenate([jnp.zeros((2, width), F32), gate_sum], axis=0)
    u0, table = project(0, qkv_xc[0], next_input)
    qkv_r.append(ring_shifted(gate(qkv_r[2], u0)))
    qkv_x.append(across(gate(qkv_r[2], u0)))
    qkv_rc.append(beside(gate(qkv_r[1], u0)))
    qkv_xc.append(beside(gate(qkv_x[1], u0)))
    kept, sent = halved(kept + gate(arrived, u0).astype(F32), 2)
    received = [sends(u0)]
    layers.append([[qkv_r[1]], [qkv_x[1]], [qkv_rc[1]], [qkv_xc[1]]])
    u1, table = project(1, qkv_xc[1], sent, received[0], next_cot)
    rest = [ring_shifted(gate(qkv_x[2], u1))]
    qkv_rc.append(beside(gate(qkv_r[2], u1)))
    qkv_rc.append(beside(gate(qkv_r[3], u1)))
    qkv_xc.append(beside(gate(qkv_x[2], u1)))
    arrived = across(gate(sent, u1))
    received.append(sends(u1))
    layers.append([[qkv_r[2]], [qkv_x[2]], [qkv_rc[2]], [qkv_xc[2]]])
    u2, table = project(2, qkv_xc[2], received[1])
    layers.append([[qkv_r[3]], rest, [qkv_rc[3]], [beside(gate(piece, u2)) for piece in rest]])
    received.append(sends(u2))
    u3, table = project(3)
    kept, sent = halved(kept + gate(arrived, u2).astype(F32), 4)
    arrived = swapped(sent, 4)
    kept, sent = halved(kept + gate(arrived, u3).astype(F32), 8)
    arrived = swapped(sent, 8)
    received.append(sends(u3))

    (passed_back,) = call(
        lambda *refs: finish_kernel(ring, *refs),
        [shape(rows, width)],
        "svv" + "v" * ring,
        [place, next_input, next_cot, *received],
        4,
        scratch=[pltpu.VMEM((rows, width), F32)],
        name="finish",
    )
    table_sum = exchanged_sum(table, passed_back)
    adapter_sum = (kept + gate(arrived, passed_back).astype(F32))[0]
    return (passed_back[None], (table_sum / count)[None], (adapter_sum / count)[None])


def solution(mesh):
    placed = (
        P("pipe", "dp", None),
        P("pipe", "dp", None),
        P("pipe", "dp", None),
        P("pipe", None, None),
        P("pipe", "dp", None),
        P("pipe", "dp"),
        P("pipe", "dp"),
        P("pipe", "dp", None),
        P("pipe", "dp", None),
        P("pipe", "dp", None),
        P("pipe", None, None),
    )
    return jax.shard_map(
        on_device,
        mesh=mesh,
        in_specs=placed,
        out_specs=(P("pipe", "dp", None), P("pipe", None, None), P("pipe", "dp", None)),
        check_vma=False,
    )
```
